32 devices in a mesh: groups: 2 (over y), gx: 8 (over z, x), gy: 2 (over core).
Axes of the slice: x: 2, y: 2, z: 4, core: 2. Of those that a mesh axis runs over, the one named last changes fastest.
Arguments:
- adj_tracer: float32 [20, 256, 512], P('groups', 'gx', 'gy'), parts along dimension 0, may hold values from -6 to 6
- adj_east: float32 [20, 256, 512], P('groups', 'gx', 'gy'), parts along dimension 0, may hold values from -6 to 6
- adj_north: float32 [20, 256, 512], P('groups', 'gx', 'gy'), parts along dimension 0, may hold values from -6 to 6
- flow_east: float32 [20, 256, 512], P('groups', 'gx', 'gy'), parts along dimension 0, may hold values from -0.6 to 0.6
- flow_north: float32 [20, 256, 512], P('groups', 'gx', 'gy'), parts along dimension 0, may hold values from -0.6 to 0.6
- mixing: float32 [20, 256, 512], P('groups', 'gx', 'gy'), parts along dimension 0, may hold values from 0.02 to 0.2
- buoyancy: float32 [10], replicated, may hold values from 0.2 to 0.8
- coriolis: float32 [512], P('gy'), may hold values from -0.5 to 0.5
- column_depth: int32 [512, 512], P(('groups', 'gx'), 'gy'), parts along dimension 0, may hold values from 0 to 10
- adj_surface: float32 [512, 512], P(('groups', 'gx'), 'gy'), parts along dimension 0, may hold values from -40 to 40
- surface_diag: float32 [512, 512], P(('groups', 'gx'), 'gy'), parts along dimension 0, may hold values from 0.05 to 0.5
- prior_surface: float32 [512, 512], P(('groups', 'gx'), 'gy'), parts along dimension 0, may hold values from -6 to 6
Outputs:
- tracer_out: float32 [20, 256, 512], P('groups', 'gx', 'gy'), parts along dimension 0
- east_out: float32 [20, 256, 512], P('groups', 'gx', 'gy'), parts along dimension 0
- north_out: float32 [20, 256, 512], P('groups', 'gx', 'gy'), parts along dimension 0
- surface_solution: float32 [512, 512], P(('groups', 'gx'), 'gy'), parts along dimension 0
The draws below stay inside these ranges and needn't reach their ends.
There are 2 independent parts, one for each index of `groups`. The reference program is written for one: setup_inputs(seed, part) draws one part's arguments, and reference() takes and returns one part's arrays. A program takes and returns all parts, laid end to end along the dimension named above; an argument that names none is the same for every part. Nothing has to cross between parts.
Inputs may be any that keep to these rules, and one draw needn't show every extreme that they name: `column_depth`: 0 marks a land column.
All inputs are finite; a program needn't handle non-finite values.
Results may differ from the reference program's by a relative error of at most 0.0001.
Values sent between devices are 32-bit elements; how exact they have to be, the bound alone decides.
A program may use at most 64 MiB of HBM per device.

```python
import math
import jax
import jax.numpy as jnp

NZ = 10
SUB = 3
ITERS = 3
NX = 256
NY = 512


def draw_adj_surface(key, part):
    key = jax.random.fold_in(key, 11)
    base_key, row_key = jax.random.split(key)
    columns = jnp.arange(NX, dtype=jnp.float32) / NX
    column_scale = 10.0 ** (columns - 0.5)
    row_scale = 10.0 ** (jax.random.uniform(row_key, (NY,), jnp.float32) - 0.5)
    base = jnp.clip(jax.random.normal(base_key, (NX, NY), jnp.float32), -4.0, 4.0)
    return base * column_scale[:, None] * row_scale[None, :]


def plant(array, key, low, top_value):
    longest = array.shape.index(max(array.shape))
    spots = []
    for shift in (0, 1):
        where = [jax.random.randint(jax.random.fold_in(key, axis), (), 0, length) for axis, length in enumerate(array.shape)]
        where[longest] = (where[longest] + shift) % array.shape[longest]
        spots.append(tuple(where))
    return array.at[spots[0]].set(low).at[spots[1]].set(top_value)


def levels(rng, shape, shards, least, top_value):
    gain = 1.0
    for axis_at, shards_of in shards:
        steps = jax.random.uniform(jax.random.fold_in(jax.random.fold_in(rng, 6), axis_at), (shards_of,), jnp.float32, least / len(shards), top_value / len(shards))
        gain = gain * jnp.repeat(jnp.exp(steps), shape[axis_at] // shards_of).reshape((-1,) + (1,) * (len(shape) - 1 - axis_at))
    return gain


def gaussian(rng, shape, deviation, limit, cuts=(), held_as=jnp.bfloat16):
    factor_of = levels(rng, shape, cuts, -0.22, 0.18) if cuts else 1.0
    values = jax.random.normal(rng, shape, jnp.float32) * deviation * factor_of
    return jnp.minimum(jnp.maximum(values, -limit), limit).astype(held_as)


def setup_inputs(seed: int = 0, part: int = 0) -> dict:
    splits = jax.random.split(jax.random.key(seed), 13)
    part_splits = jax.random.split(jax.random.fold_in(splits[12], part), 13)
    return {
        "adj_tracer": gaussian(part_splits[0], (NZ, NX, NY), 1.0, 6.0, ((1, 8), (2, 2)), jnp.float32),
        "adj_east": gaussian(part_splits[1], (NZ, NX, NY), 1.0, 6.0, ((1, 8), (2, 2)), jnp.float32),
        "adj_north": gaussian(part_splits[2], (NZ, NX, NY), 1.0, 6.0, ((1, 8), (2, 2)), jnp.float32),
        "flow_east": jnp.clip(jax.random.uniform(part_splits[3], (NZ, NX, NY), jnp.float32, -0.6, 0.6) * levels(part_splits[3], (NZ, NX, NY), ((1, 8), (2, 2)), -0.4, 0.0), -0.6, 0.6),
        "flow_north": jnp.clip(jax.random.uniform(part_splits[4], (NZ, NX, NY), jnp.float32, -0.6, 0.6) * levels(part_splits[4], (NZ, NX, NY), ((1, 8), (2, 2)), -0.4, 0.0), -0.6, 0.6),
        "mixing": jnp.clip(jnp.exp(math.log(0.2) - 2.3025851 * jax.random.uniform(part_splits[5], (NZ, NX, NY), jnp.float32) ** levels(part_splits[5], (NZ, NX, NY), ((1, 8), (2, 2)), -0.2, 0.2)), 0.02, 0.2),
        "buoyancy": jnp.clip(jnp.exp(jax.random.uniform(splits[6], (NZ,), jnp.float32, math.log(0.2), math.log(0.8))), 0.2, 0.8),
        "coriolis": jnp.clip(jax.random.uniform(splits[7], (NY,), jnp.float32, -0.5, 0.5) * levels(splits[7], (NY,), ((0, 2),), -0.4, 0.0), -0.5, 0.5),
        "column_depth": plant(jax.random.randint(part_splits[8], (NX, NY), 0, NZ + 1), jax.random.fold_in(part_splits[8], 1), 0, NZ).astype(jnp.int32),
        "adj_surface": draw_adj_surface(jax.random.fold_in(jax.random.fold_in(splits[12], part), 71), part),
        "surface_diag": jnp.clip(jnp.exp(math.log(0.5) - 2.3025851 * jax.random.uniform(part_splits[10], (NX, NY), jnp.float32) ** levels(part_splits[10], (NX, NY), ((0, 8), (1, 2)), -0.2, 0.2)), 0.05, 0.5),
        "prior_surface": gaussian(part_splits[11], (NX, NY), 1.0, 6.0, ((0, 8), (1, 2)), jnp.float32),
    }


STIFFNESS = 0.1


def neighbours(field):
    return (field, jnp.roll(field, -1, -2), jnp.roll(field, 1, -2), jnp.roll(field, -1, -1), jnp.roll(field, 1, -1))


def advance(moving, flow_east, flow_north, mixing, wet_mask, rotation, buoyancy):
    mix_here, mix_east, mix_west, mix_north, mix_south = neighbours(mixing)
    wet_here, wet_east, wet_west, wet_north, wet_south = neighbours(wet_mask)
    face_east = 0.5 * (mix_here + mix_east) * wet_here * wet_east
    face_west = 0.5 * (mix_west + mix_here) * wet_west * wet_here
    face_north = 0.5 * (mix_here + mix_north) * wet_here * wet_north
    face_south = 0.5 * (mix_south + mix_here) * wet_south * wet_here
    centre, east_side, west_side, north_side, south_side = neighbours(moving)
    carried = (centre + flow_east * (east_side - west_side) * 0.5 + flow_north * (north_side - south_side) * 0.5
               + face_east * (east_side - centre) + face_west * (west_side - centre)
               + face_north * (north_side - centre) + face_south * (south_side - centre))
    lifted = buoyancy[:, None, None] * (wet_here * wet_east * centre[1] - wet_west * wet_here * west_side[1]
                                        + wet_here * wet_north * centre[2] - wet_south * wet_here * south_side[2])
    tracer = wet_here * (carried[0] + lifted)
    east_new = wet_here * (carried[1] - rotation * centre[2])
    north_new = wet_here * (carried[2] + rotation * centre[1])
    return jnp.stack([tracer, east_new, north_new])


def reference(adj_tracer, adj_east, adj_north, flow_east, flow_north, mixing, buoyancy, coriolis,
              column_depth, adj_surface, surface_diag, prior_surface):
    row_index = jnp.arange(NY)
    interior = ((row_index > 0) & (row_index < NY - 1)).astype(jnp.float32)
    depth_eff = column_depth.astype(jnp.float32) * interior[None, :]
    heights = jnp.arange(NZ, dtype=jnp.float32)[:, None, None]
    wet_mask = (heights < depth_eff[None]).astype(jnp.float32)
    rotation = jnp.broadcast_to(coriolis[None, :], (NX, NY))
    moving = wet_mask[None] * jnp.stack([adj_tracer, adj_east, adj_north])
    for substep in range(SUB):
        moving = advance(moving, flow_east, flow_north, mixing, wet_mask, rotation, buoyancy)
    column_east = jnp.sum(moving[1], axis=0)
    column_north = jnp.sum(moving[2], axis=0)
    wet_column = (depth_eff > 0).astype(jnp.float32)
    right_side = wet_column * (adj_surface + 0.5 * (jnp.roll(column_east, 1, 0) - jnp.roll(column_east, -1, 0))
                               + 0.5 * (jnp.roll(column_north, 1, 1) - jnp.roll(column_north, -1, 1)))
    reach_east = STIFFNESS * jnp.sum(wet_mask * jnp.roll(wet_mask, -1, 1), axis=0)
    reach_north = STIFFNESS * jnp.sum(wet_mask * jnp.roll(wet_mask, -1, 2), axis=0)
    reach_west = jnp.roll(reach_east, 1, 0)
    reach_south = jnp.roll(reach_north, 1, 1)

    def surface_operator(field):
        return (surface_diag * field + reach_east * (field - jnp.roll(field, -1, 0))
                + reach_west * (field - jnp.roll(field, 1, 0))
                + reach_north * (field - jnp.roll(field, -1, 1))
                + reach_south * (field - jnp.roll(field, 1, 1)))

    solution = wet_column * prior_surface
    residual = right_side - surface_operator(solution)
    direction = residual
    norm_now = jnp.sum(residual * residual)
    for iteration in range(ITERS):
        mapped = surface_operator(direction)
        step_size = norm_now / jnp.sum(direction * mapped)
        solution = solution + step_size * direction
        residual = residual - step_size * mapped
        norm_next = jnp.sum(residual * residual)
        direction = residual + (norm_next / norm_now) * direction
        norm_now = norm_next
    grad_east = 0.5 * (jnp.roll(solution, -1, 0) - jnp.roll(solution, 1, 0))
    grad_north = 0.5 * (jnp.roll(solution, -1, 1) - jnp.roll(solution, 1, 1))
    east_out = moving[1] + wet_mask * grad_east[None]
    north_out = moving[2] + wet_mask * grad_north[None]
    return moving[0], east_out, north_out, solution
```

```python
import functools

import jax
import jax.numpy as jnp
from jax import lax
from jax.experimental import pallas as pl
from jax.experimental.pallas import tpu as pltpu
from jax.sharding import PartitionSpec as P

SUB = 3
STIFFNESS = 0.1
MESH = pl.DeviceIdType.MESH


def kernel(
    count_x,
    tracer_in, east_in, north_in, flow_e, flow_n, mixing, buoyancy, coriolis,
    depth_in, adj_surface, surface_diag, prior,
    tracer_out, east_out, north_out, solution_out,
    rows_send, rows_recv,
    corner_send, corner_recv,
    side_recv,
    plane_rows_send, plane_rows_recv, plane_corner_recv, plane_side_send, plane_side_recv,
    sum_rows_send, sum_rows_recv, sum_corner_recv, sum_side_send, sum_side_recv,
    columns, moments,
    rows_ss, rows_rs, corner_ss, corner_rs, side_ss, side_rs,
    plane_ss, plane_rs, sum_ss, sum_rs, moment_ss, moment_rs,
):
    levels, cols, lanes = tracer_in.shape
    wide = lanes + 128
    tall = cols + 8
    group = lax.axis_index("groups")
    gx = lax.axis_index("gx")
    gy = lax.axis_index("gy")
    other = 1 - gy
    east_of = lax.rem(gx + 1, count_x)
    west_of = lax.rem(gx + count_x - 1, count_x)
    targets = (west_of, east_of)
    edge = pl.multiple_of(other * (lanes - 128), 128)
    me = gx * 2 + gy
    peers = 2 * count_x

    barrier = pltpu.get_barrier_semaphore()

    @pl.loop(1, peers)
    def _(step):
        peer = lax.rem(me + step, peers)
        pl.semaphore_signal(
            barrier, inc=1, device_id=(group, peer // 2, lax.rem(peer, 2)), device_id_type=MESH
        )

    sub8 = lax.broadcasted_iota(jnp.int32, (8, 1), 0)
    lane128 = lax.broadcasted_iota(jnp.int32, (1, 128), 1)

    def roll(x, shift, axis):
        return pltpu.roll(x, shift % x.shape[axis], axis)

    row = lax.broadcasted_iota(jnp.int32, (1, lanes), 1) + gy * lanes
    inside = ((row > 0) & (row < 2 * lanes - 1)).astype(jnp.float32)
    depth_own = depth_in[...].astype(jnp.float32) * inside
    planes = (depth_own, adj_surface[...], surface_diag[...], prior[...])

    def pack_pair(first, second, side):
        if side == 0:
            return jnp.where(sub8 < 4, first[:8], roll(second[:8], 4, 0))
        return jnp.where(sub8 >= 4, first[-8:], roll(second[-8:], 4, 0))

    for side in range(2):
        plane_rows_send[side, 0:8, :] = pack_pair(planes[0], planes[1], side)
        plane_rows_send[side, 8:16, :] = pack_pair(planes[2], planes[3], side)

    def edge_tile(x):
        return jnp.where(gy == 0, x[:, lanes - 128:], x[:, :128])

    for i, plane in enumerate(planes):
        plane_side_send[i] = edge_tile(plane)
    plane_side_send[4] = jnp.broadcast_to(edge_tile(coriolis[...]), (cols, 128))

    first_lane = other * 125
    edge_lane = (lane128 >= first_lane) & (lane128 < first_lane + 3)
    corner_send[...] = jnp.zeros_like(corner_send)

    def pack_three(first, second, two, k, side):
        if side == 0:
            a, b, c = first[k, 0:8, :], second[k, 0:8, :], two[k, 0:8, :]
            return jnp.where(sub8 < 3, a, jnp.where(sub8 < 6, roll(b, 3, 0), roll(c, 6, 0)))
        a, b, c = (r[k, cols - 8:cols, :] for r in (first, second, two))
        return jnp.where(sub8 >= 5, a, jnp.where(sub8 >= 2, roll(b, 5, 0), roll(c, 2, 0)))

    @pl.loop(0, levels)
    def _(k):
        for side in range(2):
            packed = jnp.concatenate(
                [
                    pack_three(tracer_in, east_in, flow_e, k, side),
                    pack_three(north_in, mixing, flow_n, k, side),
                ],
                axis=0,
            )
            rows_send[side, k] = packed
            tile = jnp.where(edge_lane, edge_tile(packed), 0.0)
            corner_send[side] = corner_send[side] + pltpu.roll(tile, 3 * k, 1)

    def remote(src, dst, ss, rs, x, y):
        return pltpu.make_async_remote_copy(
            src_ref=src, dst_ref=dst, send_sem=ss, recv_sem=rs,
            device_id=(group, x, y), device_id_type=MESH,
        )

    def planes_copies():
        out = [remote(plane_side_send, plane_side_recv, plane_ss.at[4], plane_rs.at[4], gx, other)]
        for side in range(2):
            out.append(remote(plane_rows_send.at[side], plane_rows_recv.at[side],
                              plane_ss.at[side], plane_rs.at[side], targets[side], gy))
            out.append(remote(plane_rows_send.at[side, :, pl.ds(edge, 128)], plane_corner_recv.at[side],
                              plane_ss.at[2 + side], plane_rs.at[2 + side], targets[side], other))
        return out

    def corner_copies():
        return [remote(corner_send.at[side], corner_recv.at[side], corner_ss.at[side],
                       corner_rs.at[side], targets[side], other) for side in range(2)]

    def side_copies():
        return [remote(ref.at[:, :, pl.ds(edge, 128)], side_recv.at[i], side_ss.at[i], side_rs.at[i], gx, other)
                for i, ref in enumerate((tracer_in, east_in, north_in, mixing, flow_e, flow_n))]

    def rows_copies(k):
        return [remote(rows_send.at[side, k], rows_recv.at[side, k], rows_ss.at[side, k],
                       rows_rs.at[side, k], targets[side], gy) for side in range(2)]

    def sums_copies():
        out = [remote(sum_side_send, sum_side_recv, sum_ss.at[4], sum_rs.at[4], gx, other)]
        for side in range(2):
            out.append(remote(sum_rows_send.at[side], sum_rows_recv.at[side],
                              sum_ss.at[side], sum_rs.at[side], targets[side], gy))
            out.append(remote(sum_rows_send.at[side, :, pl.ds(edge, 128)], sum_corner_recv.at[side],
                              sum_ss.at[2 + side], sum_rs.at[2 + side], targets[side], other))
        return out

    pl.semaphore_wait(barrier, peers - 1)
    for copy in planes_copies() + corner_copies() + side_copies():
        copy.start()

    @pl.loop(0, levels)
    def _(k):
        for copy in rows_copies(k):
            copy.start()

    columns[...] = jnp.zeros_like(columns)
    for copy in planes_copies() + corner_copies() + side_copies():
        copy.wait_recv()

    def to_east(x):
        return pltpu.roll(x, tall - 1, 0)

    def to_west(x):
        return pltpu.roll(x, 1, 0)

    def to_north(x):
        return pltpu.roll(x, wide - 1, 1)

    def to_south(x):
        return pltpu.roll(x, 1, 1)

    def assemble(own, side, halo):
        return jnp.concatenate([jnp.concatenate([own, side], axis=1), halo], axis=0)

    def halo_pair(rows, corner, first):
        e = jnp.concatenate([rows[0], corner[0]], axis=1)
        w = jnp.concatenate([rows[1], corner[1]], axis=1)
        both = jnp.where(sub8 < 4, e, w) if first else jnp.where(sub8 < 4, roll(e, 4, 0), roll(w, 4, 0))
        return both

    def plane_at(i):
        tile = slice(8 * (i // 2), 8 * (i // 2) + 8)
        halo = halo_pair(
            (plane_rows_recv[0, tile, :], plane_rows_recv[1, tile, :]),
            (plane_corner_recv[0, tile, :], plane_corner_recv[1, tile, :]),
            i % 2 == 0,
        )
        return assemble(planes[i], plane_side_recv[i], halo)

    depth = plane_at(0)
    rotation = jnp.concatenate([coriolis[...], plane_side_recv[4, 0:1, :]], axis=1)

    @pl.loop(0, levels)
    def _(k):
        for copy in rows_copies(k):
            copy.wait_recv()
        back = lax.rem(128 - 3 * k, 128)
        packed = [
            jnp.concatenate([rows_recv[side, k], pltpu.roll(corner_recv[side], back, 1)], axis=1)
            for side in range(2)
        ]

        def field(ref, i, tile, shift_e, shift_w):
            e = packed[0][8 * tile:8 * tile + 8]
            w = packed[1][8 * tile:8 * tile + 8]
            halo = jnp.where(sub8 < 4, roll(e, shift_e, 0), roll(w, shift_w, 0))
            return assemble(ref[k], side_recv[i, k], halo)

        wet = (k.astype(jnp.float32) < depth).astype(jnp.float32)
        wet_e, wet_n = to_east(wet) * wet, to_north(wet) * wet
        half_mix = 0.5 * field(mixing, 3, 1, 5, 3)
        face_e = (half_mix + to_east(half_mix)) * wet_e
        face_n = (half_mix + to_north(half_mix)) * wet_n
        face_w, face_s = to_west(face_e), to_south(face_n)
        half = 0.5 * wet
        carry_e = half * field(flow_e, 4, 0, 2, 6)
        carry_n = half * field(flow_n, 5, 1, 2, 6)
        take_e, take_w = face_e + carry_e, face_w - carry_e
        take_n, take_s = face_n + carry_n, face_s - carry_n
        take = wet - (face_e + face_w) - (face_n + face_s)
        turn = wet * rotation
        lift = buoyancy[k]
        lift_e, lift_n, lift_here = lift * wet_e, lift * wet_n, lift * wet
        t = wet * field(tracer_in, 0, 0, 0, 0)
        e = wet * field(east_in, 1, 0, 5, 3)
        n = wet * field(north_in, 2, 1, 0, 0)
        for _ in range(SUB):
            e_w, n_s = to_west(e), to_south(n)
            t_new = (take * t + take_e * to_east(t) + take_w * to_west(t)
                     + take_n * to_north(t) + take_s * to_south(t)
                     + (lift_e * e + lift_n * n - lift_here * (e_w + n_s)))
            e_new = (take * e + take_e * to_east(e) + take_w * e_w
                     + take_n * to_north(e) + take_s * to_south(e) - turn * n)
            n_new = (take * n + take_e * to_east(n) + take_w * to_west(n)
                     + take_n * to_north(n) + take_s * n_s + turn * e)
            t, e, n = t_new, e_new, n_new
        own = (slice(0, cols), slice(0, lanes))
        tracer_out[k] = t[own]
        east_out[k] = e[own]
        north_out[k] = n[own]
        columns[0] = columns[0] + e[own]
        columns[1] = columns[1] + n[own]

    sum_e, sum_n = columns[0], columns[1]
    for side in range(2):
        sum_rows_send[side] = pack_pair(sum_e, sum_n, side)
    sum_side_send[0] = edge_tile(sum_e)
    sum_side_send[1] = edge_tile(sum_n)
    for copy in sums_copies():
        copy.start()

    wet_column = (depth > 0.0).astype(jnp.float32)
    reach_e = STIFFNESS * jnp.minimum(depth, to_east(depth))
    reach_n = STIFFNESS * jnp.minimum(depth, to_north(depth))
    reach_w, reach_s = to_west(reach_e), to_south(reach_n)
    centre = plane_at(2) + (reach_e + reach_w) + (reach_n + reach_s)

    def operator(p):
        return (centre * p - reach_e * to_east(p) - reach_w * to_west(p)
                - reach_n * to_north(p) - reach_s * to_south(p))

    start = wet_column * plane_at(3)
    base = wet_column * plane_at(1) - operator(start)

    for copy in sums_copies():
        copy.wait_recv()

    def sum_at(i, own):
        halo = halo_pair((sum_rows_recv[0], sum_rows_recv[1]), (sum_corner_recv[0], sum_corner_recv[1]), i == 0)
        return assemble(own, sum_side_recv[i], halo)

    all_e, all_n = sum_at(0, sum_e), sum_at(1, sum_n)
    v0 = base + (0.5 * wet_column) * (to_west(all_e) - to_east(all_e) + to_south(all_n) - to_north(all_n))
    v1 = operator(v0)
    v2 = operator(v1)
    v3 = operator(v2)

    w = [v[0:cols, 0:lanes] for v in (v0, v1, v2, v3)]

    def partial(a, b):
        s = jnp.sum((a * b).reshape(cols // 8, 8, lanes), axis=0)
        total = s[:, 0:128]
        for j in range(128, lanes, 128):
            total = total + s[:, j:j + 128]
        return jnp.sum(total, axis=0, keepdims=True)

    terms = [partial(w[0], w[0]), partial(w[0], w[1]), partial(w[1], w[1]),
             partial(w[1], w[2]), partial(w[2], w[2]), partial(w[2], w[3])]
    mine = jnp.concatenate(terms + [jnp.zeros((2, 128), jnp.float32)], axis=0)
    moments[me] = mine

    def moment_copy(step):
        peer = lax.rem(me + step, peers)
        return remote(moments.at[me], moments.at[me], moment_ss.at[step], moment_rs.at[me],
                      peer // 2, lax.rem(peer, 2))

    @pl.loop(1, peers)
    def _(step):
        moment_copy(step).start()

    @pl.loop(1, peers)
    def _(step):
        source = lax.rem(me + step, peers)
        remote(moments.at[me], moments.at[source], moment_ss.at[step], moment_rs.at[source],
               source // 2, lax.rem(source, 2)).wait_recv()

    total = jnp.sum(jnp.sum(moments[...], axis=0), axis=1, keepdims=True)
    mu = [jnp.broadcast_to(total[m:m + 1, :], (1, 128)) for m in range(6)]

    def form(c, at):
        out = 0.0
        for i, a in enumerate(c):
            for j, b in enumerate(c):
                out = out + a * b * mu[at + i + j]
        return out

    r = [jnp.ones((1, 128), jnp.float32)]
    d = list(r)
    rr = mu[0]
    gain = [jnp.zeros((1, 128), jnp.float32) for _ in range(3)]
    for iteration in range(3):
        alpha = rr / form(d, 1)
        for i in range(len(d)):
            gain[i] = gain[i] + alpha * d[i]
        if iteration < 2:
            shifted = [jnp.zeros((1, 128), jnp.float32)] + d
            r = [a - alpha * b for a, b in zip(r + [jnp.zeros((1, 128), jnp.float32)], shifted)]
            new = form(r, 0)
            beta = new / rr
            d = [a + beta * b for a, b in zip(r, d + [jnp.zeros((1, 128), jnp.float32)])]
            rr = new
    gain = [g[:, 0:1] for g in gain]
    solved = start + gain[0] * v0 + gain[1] * v1 + gain[2] * v2
    solution_out[...] = solved[0:cols, 0:lanes]
    grad_e = (0.5 * (to_east(solved) - to_west(solved)))[0:cols, 0:lanes]
    grad_n = (0.5 * (to_north(solved) - to_south(solved)))[0:cols, 0:lanes]

    @pl.loop(0, levels)
    def _(k):
        wet = k.astype(jnp.float32) < depth_own
        east_out[k] = east_out[k] + jnp.where(wet, grad_e, 0.0)
        north_out[k] = north_out[k] + jnp.where(wet, grad_n, 0.0)

    for copy in planes_copies() + corner_copies() + side_copies() + sums_copies():
        copy.wait_send()

    @pl.loop(0, levels)
    def _(k):
        for copy in rows_copies(k):
            copy.wait_send()

    @pl.loop(1, peers)
    def _(step):
        moment_copy(step).wait_send()


def per_device(count_x, *args):
    levels, cols, lanes = args[0].shape
    args = list(args)
    args[7] = args[7].reshape(1, lanes)
    f32 = jnp.float32
    vmem = pl.BlockSpec(memory_space=pltpu.VMEM)
    specs = [vmem] * 12
    specs[6] = pl.BlockSpec(memory_space=pltpu.SMEM)
    peers = 2 * count_x
    dma = pltpu.SemaphoreType.DMA
    scratch = [
        pltpu.VMEM((2, levels, 16, lanes), f32), pltpu.VMEM((2, levels, 16, lanes), f32),
        pltpu.VMEM((2, 16, 128), f32), pltpu.VMEM((2, 16, 128), f32),
        pltpu.VMEM((6, levels, cols, 128), f32),
        pltpu.VMEM((2, 16, lanes), f32), pltpu.VMEM((2, 16, lanes), f32), pltpu.VMEM((2, 16, 128), f32),
        pltpu.VMEM((5, cols, 128), f32), pltpu.VMEM((5, cols, 128), f32),
        pltpu.VMEM((2, 8, lanes), f32), pltpu.VMEM((2, 8, lanes), f32), pltpu.VMEM((2, 8, 128), f32),
        pltpu.VMEM((2, cols, 128), f32), pltpu.VMEM((2, cols, 128), f32),
        pltpu.VMEM((2, cols, lanes), f32), pltpu.VMEM((peers, 8, 128), f32),
        dma((2, levels)), dma((2, levels)), dma((2,)), dma((2,)), dma((6,)), dma((6,)),
        dma((5,)), dma((5,)), dma((5,)), dma((5,)), dma((peers,)), dma((peers,)),
    ]
    volume = jax.ShapeDtypeStruct((levels, cols, lanes), f32)
    return pl.pallas_call(
        functools.partial(kernel, count_x),
        out_shape=[volume] * 3 + [jax.ShapeDtypeStruct((cols, lanes), f32)],
        in_specs=specs,
        out_specs=[vmem] * 4,
        scratch_shapes=scratch,
        compiler_params=pltpu.CompilerParams(
            collective_id=0, has_side_effects=True, vmem_limit_bytes=32 * 1024 * 1024
        ),
    )(*args)


def solution(mesh):
    volume = P("groups", "gx", "gy")
    plane = P(("groups", "gx"), "gy")
    return jax.shard_map(
        functools.partial(per_device, mesh.shape["gx"]),
        mesh=mesh,
        in_specs=(volume,) * 6 + (P(), P("gy")) + (plane,) * 4,
        out_specs=(volume,) * 3 + (plane,),
        check_vma=False,
    )
```

```python
import functools

import jax
import jax.numpy as jnp
from jax import lax
from jax.experimental import pallas as pl
from jax.experimental.pallas import tpu as pltpu
from jax.sharding import PartitionSpec as P

SUB = 3
STIFFNESS = 0.1
MESH = pl.DeviceIdType.MESH


def kernel(
    count_x,
    tracer_hbm, east_hbm, north_hbm, flow_e_hbm, flow_n_hbm, mixing_hbm, buoyancy_hbm, coriolis_hbm,
    depth_hbm, adj_surface_hbm, surface_diag_hbm, prior_hbm,
    tracer_out, east_out, north_out, solution_out, grad_e_out, grad_n_out, depth_out,
    tracer_in, east_in, north_in, flow_e, flow_n, mixing, buoyancy, coriolis,
    depth_in, adj_surface, surface_diag, prior,
    rows_send, rows_recv,
    corner_send, corner_recv,
    side_recv,
    plane_rows_send, plane_rows_recv, plane_corner_recv, plane_side_send, plane_side_recv,
    sum_rows_send, sum_rows_recv, sum_corner_recv, sum_side_send, sum_side_recv,
    columns, moments, load_sem,
    rows_ss, rows_rs, corner_ss, corner_rs, side_ss, side_rs,
    plane_ss, plane_rs, sum_ss, sum_rs, moment_ss, moment_rs,
):
    levels, cols, lanes = tracer_in.shape
    wide = lanes + 128
    tall = cols + 8
    group = lax.axis_index("groups")
    gx = lax.axis_index("gx")
    gy = lax.axis_index("gy")
    other = 1 - gy
    east_of = lax.rem(gx + 1, count_x)
    west_of = lax.rem(gx + count_x - 1, count_x)
    targets = (west_of, east_of)
    edge = pl.multiple_of(other * (lanes - 128), 128)
    me = gx * 2 + gy
    peers = 2 * count_x

    fields_hbm = (tracer_hbm, east_hbm, north_hbm, mixing_hbm, flow_e_hbm, flow_n_hbm)
    small = [
        pltpu.make_async_copy(src, dst, load_sem.at[i])
        for i, (src, dst) in enumerate([
            (depth_hbm, depth_in), (adj_surface_hbm, adj_surface), (surface_diag_hbm, surface_diag),
            (prior_hbm, prior), (coriolis_hbm, coriolis), (buoyancy_hbm, buoyancy),
        ])
    ]
    large = [
        pltpu.make_async_copy(src, dst, load_sem.at[6 + i])
        for i, (src, dst) in enumerate(zip(fields_hbm, (tracer_in, east_in, north_in, mixing, flow_e, flow_n)))
    ]
    for copy in small + large:
        copy.start()

    barrier = pltpu.get_barrier_semaphore()

    @pl.loop(1, peers)
    def _(step):
        peer = lax.rem(me + step, peers)
        pl.semaphore_signal(
            barrier, inc=1, device_id=(group, peer // 2, lax.rem(peer, 2)), device_id_type=MESH
        )

    sub8 = lax.broadcasted_iota(jnp.int32, (8, 1), 0)
    lane128 = lax.broadcasted_iota(jnp.int32, (1, 128), 1)

    def roll(x, shift, axis):
        return pltpu.roll(x, shift % x.shape[axis], axis)

    for copy in small:
        copy.wait()

    row = lax.broadcasted_iota(jnp.int32, (1, lanes), 1) + gy * lanes
    inside = ((row > 0) & (row < 2 * lanes - 1)).astype(jnp.float32)
    depth_own = depth_in[...].astype(jnp.float32) * inside
    planes = (depth_own, adj_surface[...], surface_diag[...], prior[...])

    def pack_pair(first, second, side):
        if side == 0:
            return jnp.where(sub8 < 4, first[:8], roll(second[:8], 4, 0))
        return jnp.where(sub8 >= 4, first[-8:], roll(second[-8:], 4, 0))

    for side in range(2):
        plane_rows_send[side, 0:8, :] = pack_pair(planes[0], planes[1], side)
        plane_rows_send[side, 8:16, :] = pack_pair(planes[2], planes[3], side)

    def edge_tile(x):
        return jnp.where(gy == 0, x[:, lanes - 128:], x[:, :128])

    for i, plane in enumerate(planes):
        plane_side_send[i] = edge_tile(plane)
    plane_side_send[4] = jnp.broadcast_to(edge_tile(coriolis[...]), (cols, 128))

    first_lane = other * 125
    edge_lane = (lane128 >= first_lane) & (lane128 < first_lane + 3)
    corner_send[...] = jnp.zeros_like(corner_send)

    def pack_three(first, second, two, k, side):
        if side == 0:
            a, b, c = first[k, 0:8, :], second[k, 0:8, :], two[k, 0:8, :]
            return jnp.where(sub8 < 3, a, jnp.where(sub8 < 6, roll(b, 3, 0), roll(c, 6, 0)))
        a, b, c = (r[k, cols - 8:cols, :] for r in (first, second, two))
        return jnp.where(sub8 >= 5, a, jnp.where(sub8 >= 2, roll(b, 5, 0), roll(c, 2, 0)))

    def remote(src, dst, ss, rs, x, y):
        return pltpu.make_async_remote_copy(
            src_ref=src, dst_ref=dst, send_sem=ss, recv_sem=rs,
            device_id=(group, x, y), device_id_type=MESH,
        )

    def planes_copies():
        out = [remote(plane_side_send, plane_side_recv, plane_ss.at[4], plane_rs.at[4], gx, other)]
        for side in range(2):
            out.append(remote(plane_rows_send.at[side], plane_rows_recv.at[side],
                              plane_ss.at[side], plane_rs.at[side], targets[side], gy))
            out.append(remote(plane_rows_send.at[side, :, pl.ds(edge, 128)], plane_corner_recv.at[side],
                              plane_ss.at[2 + side], plane_rs.at[2 + side], targets[side], other))
        return out

    def corner_copies():
        return [remote(corner_send.at[side], corner_recv.at[side], corner_ss.at[side],
                       corner_rs.at[side], targets[side], other) for side in range(2)]

    def side_copies():
        return [remote(ref.at[:, :, pl.ds(edge, 128)], side_recv.at[i], side_ss.at[i], side_rs.at[i], gx, other)
                for i, ref in enumerate(fields_hbm)]

    def rows_copies(k):
        return [remote(rows_send.at[side, k], rows_recv.at[side, k], rows_ss.at[side, k],
                       rows_rs.at[side, k], targets[side], gy) for side in range(2)]

    def sums_copies():
        out = [remote(sum_side_send, sum_side_recv, sum_ss.at[4], sum_rs.at[4], gx, other)]
        for side in range(2):
            out.append(remote(sum_rows_send.at[side], sum_rows_recv.at[side],
                              sum_ss.at[side], sum_rs.at[side], targets[side], gy))
            out.append(remote(sum_rows_send.at[side, :, pl.ds(edge, 128)], sum_corner_recv.at[side],
                              sum_ss.at[2 + side], sum_rs.at[2 + side], targets[side], other))
        return out

    pl.semaphore_wait(barrier, peers - 1)
    for copy in planes_copies() + side_copies():
        copy.start()
    for copy in large:
        copy.wait()

    @pl.loop(0, levels)
    def _(k):
        for side in range(2):
            packed = jnp.concatenate(
                [
                    pack_three(tracer_in, east_in, flow_e, k, side),
                    pack_three(north_in, mixing, flow_n, k, side),
                ],
                axis=0,
            )
            rows_send[side, k] = packed
            tile = jnp.where(edge_lane, edge_tile(packed), 0.0)
            corner_send[side] = corner_send[side] + pltpu.roll(tile, 3 * k, 1)
        for copy in rows_copies(k):
            copy.start()

    for copy in corner_copies():
        copy.start()

    columns[...] = jnp.zeros_like(columns)
    for copy in planes_copies() + corner_copies() + side_copies():
        copy.wait_recv()

    def to_east(x):
        return pltpu.roll(x, tall - 1, 0)

    def to_west(x):
        return pltpu.roll(x, 1, 0)

    def to_north(x):
        return pltpu.roll(x, wide - 1, 1)

    def to_south(x):
        return pltpu.roll(x, 1, 1)

    def assemble(own, side, halo):
        return jnp.concatenate([jnp.concatenate([own, side], axis=1), halo], axis=0)

    def halo_pair(rows, corner, first):
        e = jnp.concatenate([rows[0], corner[0]], axis=1)
        w = jnp.concatenate([rows[1], corner[1]], axis=1)
        both = jnp.where(sub8 < 4, e, w) if first else jnp.where(sub8 < 4, roll(e, 4, 0), roll(w, 4, 0))
        return both

    def plane_at(i):
        tile = slice(8 * (i // 2), 8 * (i // 2) + 8)
        halo = halo_pair(
            (plane_rows_recv[0, tile, :], plane_rows_recv[1, tile, :]),
            (plane_corner_recv[0, tile, :], plane_corner_recv[1, tile, :]),
            i % 2 == 0,
        )
        return assemble(planes[i], plane_side_recv[i], halo)

    depth = plane_at(0)
    rotation = jnp.concatenate([coriolis[...], plane_side_recv[4, 0:1, :]], axis=1)

    @pl.loop(0, levels)
    def _(k):
        for copy in rows_copies(k):
            copy.wait_recv()
        back = lax.rem(128 - 3 * k, 128)
        packed = [
            jnp.concatenate([rows_recv[side, k], pltpu.roll(corner_recv[side], back, 1)], axis=1)
            for side in range(2)
        ]

        def field(ref, i, tile, shift_e, shift_w):
            e = packed[0][8 * tile:8 * tile + 8]
            w = packed[1][8 * tile:8 * tile + 8]
            halo = jnp.where(sub8 < 4, roll(e, shift_e, 0), roll(w, shift_w, 0))
            return assemble(ref[k], side_recv[i, k], halo)

        wet = (k.astype(jnp.float32) < depth).astype(jnp.float32)
        wet_e, wet_n = to_east(wet) * wet, to_north(wet) * wet
        half_mix = 0.5 * field(mixing, 3, 1, 5, 3)
        face_e = (half_mix + to_east(half_mix)) * wet_e
        face_n = (half_mix + to_north(half_mix)) * wet_n
        face_w, face_s = to_west(face_e), to_south(face_n)
        half = 0.5 * wet
        carry_e = half * field(flow_e, 4, 0, 2, 6)
        carry_n = half * field(flow_n, 5, 1, 2, 6)
        take_e, take_w = face_e + carry_e, face_w - carry_e
        take_n, take_s = face_n + carry_n, face_s - carry_n
        take = wet - (face_e + face_w) - (face_n + face_s)
        turn = wet * rotation
        lift = buoyancy[k]
        lift_e, lift_n, lift_here = lift * wet_e, lift * wet_n, lift * wet
        t = wet * field(tracer_in, 0, 0, 0, 0)
        e = wet * field(east_in, 1, 0, 5, 3)
        n = wet * field(north_in, 2, 1, 0, 0)
        for _ in range(SUB):
            e_w, n_s = to_west(e), to_south(n)
            t_new = (take * t + take_e * to_east(t) + take_w * to_west(t)
                     + take_n * to_north(t) + take_s * to_south(t)
                     + (lift_e * e + lift_n * n - lift_here * (e_w + n_s)))
            e_new = (take * e + take_e * to_east(e) + take_w * e_w
                     + take_n * to_north(e) + take_s * to_south(e) - turn * n)
            n_new = (take * n + take_e * to_east(n) + take_w * to_west(n)
                     + take_n * to_north(n) + take_s * n_s + turn * e)
            t, e, n = t_new, e_new, n_new
        own = (slice(0, cols), slice(0, lanes))
        tracer_out[k] = t[own]
        east_out[k] = e[own]
        north_out[k] = n[own]
        columns[0] = columns[0] + e[own]
        columns[1] = columns[1] + n[own]

    sum_e, sum_n = columns[0], columns[1]
    for side in range(2):
        sum_rows_send[side] = pack_pair(sum_e, sum_n, side)
    sum_side_send[0] = edge_tile(sum_e)
    sum_side_send[1] = edge_tile(sum_n)
    for copy in sums_copies():
        copy.start()

    wet_column = (depth > 0.0).astype(jnp.float32)
    reach_e = STIFFNESS * jnp.minimum(depth, to_east(depth))
    reach_n = STIFFNESS * jnp.minimum(depth, to_north(depth))
    reach_w, reach_s = to_west(reach_e), to_south(reach_n)
    centre = plane_at(2) + (reach_e + reach_w) + (reach_n + reach_s)

    def operator(p):
        return (centre * p - reach_e * to_east(p) - reach_w * to_west(p)
                - reach_n * to_north(p) - reach_s * to_south(p))

    start = wet_column * plane_at(3)
    base = wet_column * plane_at(1) - operator(start)

    for copy in sums_copies():
        copy.wait_recv()

    def sum_at(i, own):
        halo = halo_pair((sum_rows_recv[0], sum_rows_recv[1]), (sum_corner_recv[0], sum_corner_recv[1]), i == 0)
        return assemble(own, sum_side_recv[i], halo)

    all_e, all_n = sum_at(0, sum_e), sum_at(1, sum_n)
    v0 = base + (0.5 * wet_column) * (to_west(all_e) - to_east(all_e) + to_south(all_n) - to_north(all_n))
    v1 = operator(v0)
    v2 = operator(v1)
    v3 = operator(v2)

    w = [v[0:cols, 0:lanes] for v in (v0, v1, v2, v3)]

    def partial(a, b):
        s = jnp.sum((a * b).reshape(cols // 8, 8, lanes), axis=0)
        total = s[:, 0:128]
        for j in range(128, lanes, 128):
            total = total + s[:, j:j + 128]
        return jnp.sum(total, axis=0, keepdims=True)

    terms = [partial(w[0], w[0]), partial(w[0], w[1]), partial(w[1], w[1]),
             partial(w[1], w[2]), partial(w[2], w[2]), partial(w[2], w[3])]
    mine = jnp.concatenate(terms + [jnp.zeros((2, 128), jnp.float32)], axis=0)
    moments[me] = mine

    def moment_copy(step):
        peer = lax.rem(me + step, peers)
        return remote(moments.at[me], moments.at[me], moment_ss.at[step], moment_rs.at[me],
                      peer // 2, lax.rem(peer, 2))

    @pl.loop(1, peers)
    def _(step):
        moment_copy(step).start()

    @pl.loop(1, peers)
    def _(step):
        source = lax.rem(me + step, peers)
        remote(moments.at[me], moments.at[source], moment_ss.at[step], moment_rs.at[source],
               source // 2, lax.rem(source, 2)).wait_recv()

    total = jnp.sum(jnp.sum(moments[...], axis=0), axis=1, keepdims=True)
    mu = [jnp.broadcast_to(total[m:m + 1, :], (1, 128)) for m in range(6)]

    def form(c, at):
        out = 0.0
        for i, a in enumerate(c):
            for j, b in enumerate(c):
                out = out + a * b * mu[at + i + j]
        return out

    r = [jnp.ones((1, 128), jnp.float32)]
    d = list(r)
    rr = mu[0]
    gain = [jnp.zeros((1, 128), jnp.float32) for _ in range(3)]
    for iteration in range(3):
        alpha = rr / form(d, 1)
        for i in range(len(d)):
            gain[i] = gain[i] + alpha * d[i]
        if iteration < 2:
            shifted = [jnp.zeros((1, 128), jnp.float32)] + d
            r = [a - alpha * b for a, b in zip(r + [jnp.zeros((1, 128), jnp.float32)], shifted)]
            new = form(r, 0)
            beta = new / rr
            d = [a + beta * b for a, b in zip(r, d + [jnp.zeros((1, 128), jnp.float32)])]
            rr = new
    gain = [g[:, 0:1] for g in gain]
    solved = start + gain[0] * v0 + gain[1] * v1 + gain[2] * v2
    solution_out[...] = solved[0:cols, 0:lanes]
    grad_e_out[...] = (0.5 * (to_east(solved) - to_west(solved)))[0:cols, 0:lanes]
    grad_n_out[...] = (0.5 * (to_north(solved) - to_south(solved)))[0:cols, 0:lanes]
    depth_out[...] = depth_own

    for copy in planes_copies() + corner_copies() + side_copies() + sums_copies():
        copy.wait_send()

    @pl.loop(0, levels)
    def _(k):
        for copy in rows_copies(k):
            copy.wait_send()

    @pl.loop(1, peers)
    def _(step):
        moment_copy(step).wait_send()


def per_device(count_x, *args):
    levels, cols, lanes = args[0].shape
    args = list(args)
    args[7] = args[7].reshape(1, lanes)
    f32 = jnp.float32
    vmem = pl.BlockSpec(memory_space=pltpu.VMEM)
    hbm = pl.BlockSpec(memory_space=pltpu.HBM)
    peers = 2 * count_x
    dma = pltpu.SemaphoreType.DMA
    scratch = [pltpu.VMEM((levels, cols, lanes), f32)] * 6 + [
        pltpu.SMEM((levels,), f32), pltpu.VMEM((1, lanes), f32), pltpu.VMEM((cols, lanes), args[8].dtype),
    ] + [pltpu.VMEM((cols, lanes), f32)] * 3 + [
        pltpu.VMEM((2, levels, 16, lanes), f32), pltpu.VMEM((2, levels, 16, lanes), f32),
        pltpu.VMEM((2, 16, 128), f32), pltpu.VMEM((2, 16, 128), f32),
        pltpu.VMEM((6, levels, cols, 128), f32),
        pltpu.VMEM((2, 16, lanes), f32), pltpu.VMEM((2, 16, lanes), f32), pltpu.VMEM((2, 16, 128), f32),
        pltpu.VMEM((5, cols, 128), f32), pltpu.VMEM((5, cols, 128), f32),
        pltpu.VMEM((2, 8, lanes), f32), pltpu.VMEM((2, 8, lanes), f32), pltpu.VMEM((2, 8, 128), f32),
        pltpu.VMEM((2, cols, 128), f32), pltpu.VMEM((2, cols, 128), f32),
        pltpu.VMEM((2, cols, lanes), f32), pltpu.VMEM((peers, 8, 128), f32), dma((12,)),
        dma((2, levels)), dma((2, levels)), dma((2,)), dma((2,)), dma((6,)), dma((6,)),
        dma((5,)), dma((5,)), dma((5,)), dma((5,)), dma((peers,)), dma((peers,)),
    ]
    volume = jax.ShapeDtypeStruct((levels, cols, lanes), f32)
    plane = jax.ShapeDtypeStruct((cols, lanes), f32)
    tracer, east, north, solved, grad_e, grad_n, depth = pl.pallas_call(
        functools.partial(kernel, count_x),
        out_shape=[volume] * 3 + [plane] * 4,
        in_specs=[hbm] * 12,
        out_specs=[vmem] * 7,
        scratch_shapes=scratch,
        compiler_params=pltpu.CompilerParams(
            collective_id=0, has_side_effects=True, vmem_limit_bytes=60 * 1024 * 1024
        ),
    )(*args)
    wet = (jnp.arange(levels, dtype=f32)[:, None, None] < depth[None]).astype(f32)
    return wet * tracer, east + wet * grad_e, north + wet * grad_n, solved


def solution(mesh):
    volume = P("groups", "gx", "gy")
    plane = P(("groups", "gx"), "gy")
    return jax.shard_map(
        functools.partial(per_device, mesh.shape["gx"]),
        mesh=mesh,
        in_specs=(volume,) * 6 + (P(), P("gy")) + (plane,) * 4,
        out_specs=(volume,) * 3 + (plane,),
        check_vma=False,
    )
```

```python
import functools

import jax
import jax.numpy as jnp
from jax import lax
from jax.experimental import pallas as pl
from jax.experimental.pallas import tpu as pltpu
from jax.sharding import PartitionSpec as P

SUB = 3
STIFFNESS = 0.1
WINDOW = 6
MESH = pl.DeviceIdType.MESH


def kernel(
    count_x,
    tracer_hbm, east_hbm, north_hbm, flow_e_hbm, flow_n_hbm, mixing_hbm, buoyancy_hbm, coriolis_hbm,
    depth_hbm, adj_surface_hbm, surface_diag_hbm, prior_hbm,
    tracer_out, east_out, north_out, solution_out, grad_e_out, grad_n_out, depth_out,
    tracer_in, east_in, north_in, flow_e, flow_n, mixing, buoyancy, coriolis,
    depth_in, adj_surface, surface_diag, prior,
    rows_send, rows_recv,
    corner_send, corner_recv,
    side_recv,
    plane_rows_send, plane_rows_recv, plane_corner_recv, plane_side_send, plane_side_recv,
    sum_rows_send, sum_rows_recv, sum_corner_recv, sum_side_send, sum_side_recv,
    columns, moments, load_sem,
    rows_ss, rows_rs, corner_ss, corner_rs, side_ss, side_rs,
    plane_ss, plane_rs, sum_ss, sum_rs, moment_ss, moment_rs,
):
    levels, cols, lanes = tracer_in.shape
    wide = lanes + 128
    tall = cols + 8
    group = lax.axis_index("groups")
    gx = lax.axis_index("gx")
    gy = lax.axis_index("gy")
    other = 1 - gy
    east_of = lax.rem(gx + 1, count_x)
    west_of = lax.rem(gx + count_x - 1, count_x)
    targets = (west_of, east_of)
    edge = pl.multiple_of(other * (lanes - 128), 128)
    me = gx * 2 + gy
    peers = 2 * count_x
    window = min(WINDOW, levels)

    barrier = pltpu.get_barrier_semaphore()

    @pl.loop(1, peers)
    def _(step):
        peer = lax.rem(me + step, peers)
        pl.semaphore_signal(
            barrier, inc=1, device_id=(group, peer // 2, lax.rem(peer, 2)), device_id_type=MESH
        )

    fields_hbm = (tracer_hbm, east_hbm, north_hbm, mixing_hbm, flow_e_hbm, flow_n_hbm)
    small = [
        pltpu.make_async_copy(src, dst, load_sem.at[i])
        for i, (src, dst) in enumerate([
            (depth_hbm, depth_in), (adj_surface_hbm, adj_surface), (surface_diag_hbm, surface_diag),
            (prior_hbm, prior), (coriolis_hbm, coriolis), (buoyancy_hbm, buoyancy),
        ])
    ]
    large = [
        pltpu.make_async_copy(src, dst, load_sem.at[6 + i])
        for i, (src, dst) in enumerate(zip(fields_hbm, (tracer_in, east_in, north_in, mixing, flow_e, flow_n)))
    ]
    for copy in small + large:
        copy.start()

    sub8 = lax.broadcasted_iota(jnp.int32, (8, 1), 0)
    lane128 = lax.broadcasted_iota(jnp.int32, (1, 128), 1)

    def roll(x, shift, axis):
        return pltpu.roll(x, shift % x.shape[axis], axis)

    for copy in small:
        copy.wait()

    row = lax.broadcasted_iota(jnp.int32, (1, lanes), 1) + gy * lanes
    inside = ((row > 0) & (row < 2 * lanes - 1)).astype(jnp.float32)
    depth_own = depth_in[...].astype(jnp.float32) * inside
    planes = (depth_own, adj_surface[...], surface_diag[...], prior[...])

    def pack_pair(first, second, side):
        if side == 0:
            return jnp.where(sub8 < 4, first[:8], roll(second[:8], 4, 0))
        return jnp.where(sub8 >= 4, first[-8:], roll(second[-8:], 4, 0))

    for side in range(2):
        plane_rows_send[side, 0:8, :] = pack_pair(planes[0], planes[1], side)
        plane_rows_send[side, 8:16, :] = pack_pair(planes[2], planes[3], side)

    def edge_tile(x):
        return jnp.where(gy == 0, x[:, lanes - 128:], x[:, :128])

    for i, plane in enumerate(planes):
        plane_side_send[i] = edge_tile(plane)
    plane_side_send[4] = jnp.broadcast_to(edge_tile(coriolis[...]), (cols, 128))

    first_lane = other * 125
    edge_lane = (lane128 >= first_lane) & (lane128 < first_lane + 3)
    corner_send[...] = jnp.zeros_like(corner_send)

    def pack_three(first, second, two, k, side):
        if side == 0:
            a, b, c = first[k, 0:8, :], second[k, 0:8, :], two[k, 0:8, :]
            return jnp.where(sub8 < 3, a, jnp.where(sub8 < 6, roll(b, 3, 0), roll(c, 6, 0)))
        a, b, c = (r[k, cols - 8:cols, :] for r in (first, second, two))
        return jnp.where(sub8 >= 5, a, jnp.where(sub8 >= 2, roll(b, 5, 0), roll(c, 2, 0)))

    def remote(src, dst, ss, rs, x, y):
        return pltpu.make_async_remote_copy(
            src_ref=src, dst_ref=dst, send_sem=ss, recv_sem=rs,
            device_id=(group, x, y), device_id_type=MESH,
        )

    def planes_copies():
        out = [remote(plane_side_send, plane_side_recv, plane_ss.at[4], plane_rs.at[4], gx, other)]
        for side in range(2):
            out.append(remote(plane_rows_send.at[side], plane_rows_recv.at[side],
                              plane_ss.at[side], plane_rs.at[side], targets[side], gy))
            out.append(remote(plane_rows_send.at[side, :, pl.ds(edge, 128)], plane_corner_recv.at[side],
                              plane_ss.at[2 + side], plane_rs.at[2 + side], targets[side], other))
        return out

    def corner_copies():
        return [remote(corner_send.at[side], corner_recv.at[side], corner_ss.at[side],
                       corner_rs.at[side], targets[side], other) for side in range(2)]

    def side_copies():
        return [remote(ref.at[:, :, pl.ds(edge, 128)], side_recv.at[i], side_ss.at[i], side_rs.at[i], gx, other)
                for i, ref in enumerate(fields_hbm)]

    def rows_copies(k):
        return [remote(rows_send.at[side, k], rows_recv.at[side, k], rows_ss.at[side, k],
                       rows_rs.at[side, k], targets[side], gy) for side in range(2)]

    def sums_copies():
        out = [remote(sum_side_send, sum_side_recv, sum_ss.at[4], sum_rs.at[4], gx, other)]
        for side in range(2):
            out.append(remote(sum_rows_send.at[side], sum_rows_recv.at[side],
                              sum_ss.at[side], sum_rs.at[side], targets[side], gy))
            out.append(remote(sum_rows_send.at[side, :, pl.ds(edge, 128)], sum_corner_recv.at[side],
                              sum_ss.at[2 + side], sum_rs.at[2 + side], targets[side], other))
        return out

    pl.semaphore_wait(barrier, peers - 1)
    for copy in planes_copies() + side_copies():
        copy.start()
    for copy in large:
        copy.wait()

    @pl.loop(0, levels)
    def _(k):
        for side in range(2):
            packed = jnp.concatenate(
                [
                    pack_three(tracer_in, east_in, flow_e, k, side),
                    pack_three(north_in, mixing, flow_n, k, side),
                ],
                axis=0,
            )
            rows_send[side, k] = packed
            tile = jnp.where(edge_lane, edge_tile(packed), 0.0)
            corner_send[side] = corner_send[side] + pltpu.roll(tile, 3 * k, 1)

    for copy in corner_copies():
        copy.start()

    @pl.loop(0, window)
    def _(k):
        for copy in rows_copies(k):
            copy.start()

    columns[...] = jnp.zeros_like(columns)
    for copy in planes_copies() + corner_copies() + side_copies():
        copy.wait_recv()

    def to_east(x):
        return pltpu.roll(x, tall - 1, 0)

    def to_west(x):
        return pltpu.roll(x, 1, 0)

    def to_north(x):
        return pltpu.roll(x, wide - 1, 1)

    def to_south(x):
        return pltpu.roll(x, 1, 1)

    def assemble(own, side, halo):
        return jnp.concatenate([jnp.concatenate([own, side], axis=1), halo], axis=0)

    def halo_pair(rows, corner, first):
        e = jnp.concatenate([rows[0], corner[0]], axis=1)
        w = jnp.concatenate([rows[1], corner[1]], axis=1)
        both = jnp.where(sub8 < 4, e, w) if first else jnp.where(sub8 < 4, roll(e, 4, 0), roll(w, 4, 0))
        return both

    def plane_at(i):
        tile = slice(8 * (i // 2), 8 * (i // 2) + 8)
        halo = halo_pair(
            (plane_rows_recv[0, tile, :], plane_rows_recv[1, tile, :]),
            (plane_corner_recv[0, tile, :], plane_corner_recv[1, tile, :]),
            i % 2 == 0,
        )
        return assemble(planes[i], plane_side_recv[i], halo)

    depth = plane_at(0)
    rotation = jnp.concatenate([coriolis[...], plane_side_recv[4, 0:1, :]], axis=1)

    @pl.loop(0, levels)
    def _(k):
        for copy in rows_copies(k):
            copy.wait_recv()

        @pl.when(k + window < levels)
        def _():
            for copy in rows_copies(k):
                copy.wait_send()
            for copy in rows_copies(k + window):
                copy.start()

        back = lax.rem(128 - 3 * k, 128)
        packed = [
            jnp.concatenate([rows_recv[side, k], pltpu.roll(corner_recv[side], back, 1)], axis=1)
            for side in range(2)
        ]

        def field(ref, i, tile, shift_e, shift_w):
            e = packed[0][8 * tile:8 * tile + 8]
            w = packed[1][8 * tile:8 * tile + 8]
            halo = jnp.where(sub8 < 4, roll(e, shift_e, 0), roll(w, shift_w, 0))
            return assemble(ref[k], side_recv[i, k], halo)

        wet = (k.astype(jnp.float32) < depth).astype(jnp.float32)
        wet_e, wet_n = to_east(wet) * wet, to_north(wet) * wet
        half_mix = 0.5 * field(mixing, 3, 1, 5, 3)
        face_e = (half_mix + to_east(half_mix)) * wet_e
        face_n = (half_mix + to_north(half_mix)) * wet_n
        face_w, face_s = to_west(face_e), to_south(face_n)
        half = 0.5 * wet
        carry_e = half * field(flow_e, 4, 0, 2, 6)
        carry_n = half * field(flow_n, 5, 1, 2, 6)
        take_e, take_w = face_e + carry_e, face_w - carry_e
        take_n, take_s = face_n + carry_n, face_s - carry_n
        take = wet - (face_e + face_w) - (face_n + face_s)
        turn = wet * rotation
        lift = buoyancy[k]
        lift_e, lift_n, lift_here = lift * wet_e, lift * wet_n, lift * wet
        t = wet * field(tracer_in, 0, 0, 0, 0)
        e = wet * field(east_in, 1, 0, 5, 3)
        n = wet * field(north_in, 2, 1, 0, 0)
        for _ in range(SUB):
            e_w, n_s = to_west(e), to_south(n)
            t_new = (take * t + take_e * to_east(t) + take_w * to_west(t)
                     + take_n * to_north(t) + take_s * to_south(t)
                     + (lift_e * e + lift_n * n - lift_here * (e_w + n_s)))
            e_new = (take * e + take_e * to_east(e) + take_w * e_w
                     + take_n * to_north(e) + take_s * to_south(e) - turn * n)
            n_new = (take * n + take_e * to_east(n) + take_w * to_west(n)
                     + take_n * to_north(n) + take_s * n_s + turn * e)
            t, e, n = t_new, e_new, n_new
        own = (slice(0, cols), slice(0, lanes))
        tracer_out[k] = t[own]
        east_out[k] = e[own]
        north_out[k] = n[own]
        columns[0] = columns[0] + e[own]
        columns[1] = columns[1] + n[own]

    sum_e, sum_n = columns[0], columns[1]
    for side in range(2):
        sum_rows_send[side] = pack_pair(sum_e, sum_n, side)
    sum_side_send[0] = edge_tile(sum_e)
    sum_side_send[1] = edge_tile(sum_n)
    for copy in sums_copies():
        copy.start()

    wet_column = (depth > 0.0).astype(jnp.float32)
    reach_e = STIFFNESS * jnp.minimum(depth, to_east(depth))
    reach_n = STIFFNESS * jnp.minimum(depth, to_north(depth))
    reach_w, reach_s = to_west(reach_e), to_south(reach_n)
    centre = plane_at(2) + (reach_e + reach_w) + (reach_n + reach_s)

    def operator(p):
        return (centre * p - reach_e * to_east(p) - reach_w * to_west(p)
                - reach_n * to_north(p) - reach_s * to_south(p))

    start = wet_column * plane_at(3)
    base = wet_column * plane_at(1) - operator(start)

    for copy in sums_copies():
        copy.wait_recv()

    def sum_at(i, own):
        halo = halo_pair((sum_rows_recv[0], sum_rows_recv[1]), (sum_corner_recv[0], sum_corner_recv[1]), i == 0)
        return assemble(own, sum_side_recv[i], halo)

    all_e, all_n = sum_at(0, sum_e), sum_at(1, sum_n)
    v0 = base + (0.5 * wet_column) * (to_west(all_e) - to_east(all_e) + to_south(all_n) - to_north(all_n))
    v1 = operator(v0)
    v2 = operator(v1)
    v3 = operator(v2)

    w = [v[0:cols, 0:lanes] for v in (v0, v1, v2, v3)]

    def partial(a, b):
        s = jnp.sum((a * b).reshape(cols // 8, 8, lanes), axis=0)
        total = s[:, 0:128]
        for j in range(128, lanes, 128):
            total = total + s[:, j:j + 128]
        return jnp.sum(total, axis=0, keepdims=True)

    terms = [partial(w[0], w[0]), partial(w[0], w[1]), partial(w[1], w[1]),
             partial(w[1], w[2]), partial(w[2], w[2]), partial(w[2], w[3])]
    mine = jnp.concatenate(terms + [jnp.zeros((2, 128), jnp.float32)], axis=0)
    moments[me] = mine

    def moment_copy(step):
        peer = lax.rem(me + step, peers)
        return remote(moments.at[me], moments.at[me], moment_ss.at[step], moment_rs.at[me],
                      peer // 2, lax.rem(peer, 2))

    @pl.loop(1, peers)
    def _(step):
        moment_copy(step).start()

    @pl.loop(1, peers)
    def _(step):
        source = lax.rem(me + step, peers)
        remote(moments.at[me], moments.at[source], moment_ss.at[step], moment_rs.at[source],
               source // 2, lax.rem(source, 2)).wait_recv()

    total = jnp.sum(jnp.sum(moments[...], axis=0), axis=1, keepdims=True)
    mu = [jnp.broadcast_to(total[m:m + 1, :], (1, 128)) for m in range(6)]

    def form(c, at):
        out = 0.0
        for i, a in enumerate(c):
            for j, b in enumerate(c):
                out = out + a * b * mu[at + i + j]
        return out

    r = [jnp.ones((1, 128), jnp.float32)]
    d = list(r)
    rr = mu[0]
    gain = [jnp.zeros((1, 128), jnp.float32) for _ in range(3)]
    for iteration in range(3):
        alpha = rr / form(d, 1)
        for i in range(len(d)):
            gain[i] = gain[i] + alpha * d[i]
        if iteration < 2:
            shifted = [jnp.zeros((1, 128), jnp.float32)] + d
            r = [a - alpha * b for a, b in zip(r + [jnp.zeros((1, 128), jnp.float32)], shifted)]
            new = form(r, 0)
            beta = new / rr
            d = [a + beta * b for a, b in zip(r, d + [jnp.zeros((1, 128), jnp.float32)])]
            rr = new
    gain = [g[:, 0:1] for g in gain]
    solved = start + gain[0] * v0 + gain[1] * v1 + gain[2] * v2
    solution_out[...] = solved[0:cols, 0:lanes]
    grad_e_out[...] = (0.5 * (to_east(solved) - to_west(solved)))[0:cols, 0:lanes]
    grad_n_out[...] = (0.5 * (to_north(solved) - to_south(solved)))[0:cols, 0:lanes]
    depth_out[...] = depth_own

    for copy in planes_copies() + corner_copies() + side_copies() + sums_copies():
        copy.wait_send()

    @pl.loop(levels - window, levels)
    def _(k):
        for copy in rows_copies(k):
            copy.wait_send()

    @pl.loop(1, peers)
    def _(step):
        moment_copy(step).wait_send()


def per_device(count_x, *args):
    levels, cols, lanes = args[0].shape
    args = list(args)
    args[7] = args[7].reshape(1, lanes)
    f32 = jnp.float32
    vmem = pl.BlockSpec(memory_space=pltpu.VMEM)
    hbm = pl.BlockSpec(memory_space=pltpu.HBM)
    peers = 2 * count_x
    dma = pltpu.SemaphoreType.DMA
    scratch = [pltpu.VMEM((levels, cols, lanes), f32)] * 6 + [
        pltpu.SMEM((levels,), f32), pltpu.VMEM((1, lanes), f32), pltpu.VMEM((cols, lanes), args[8].dtype),
    ] + [pltpu.VMEM((cols, lanes), f32)] * 3 + [
        pltpu.VMEM((2, levels, 16, lanes), f32), pltpu.VMEM((2, levels, 16, lanes), f32),
        pltpu.VMEM((2, 16, 128), f32), pltpu.VMEM((2, 16, 128), f32),
        pltpu.VMEM((6, levels, cols, 128), f32),
        pltpu.VMEM((2, 16, lanes), f32), pltpu.VMEM((2, 16, lanes), f32), pltpu.VMEM((2, 16, 128), f32),
        pltpu.VMEM((5, cols, 128), f32), pltpu.VMEM((5, cols, 128), f32),
        pltpu.VMEM((2, 8, lanes), f32), pltpu.VMEM((2, 8, lanes), f32), pltpu.VMEM((2, 8, 128), f32),
        pltpu.VMEM((2, cols, 128), f32), pltpu.VMEM((2, cols, 128), f32),
        pltpu.VMEM((2, cols, lanes), f32), pltpu.VMEM((peers, 8, 128), f32), dma((12,)),
        dma((2, levels)), dma((2, levels)), dma((2,)), dma((2,)), dma((6,)), dma((6,)),
        dma((5,)), dma((5,)), dma((5,)), dma((5,)), dma((peers,)), dma((peers,)),
    ]
    volume = jax.ShapeDtypeStruct((levels, cols, lanes), f32)
    plane = jax.ShapeDtypeStruct((cols, lanes), f32)
    tracer, east, north, solved, grad_e, grad_n, depth = pl.pallas_call(
        functools.partial(kernel, count_x),
        out_shape=[volume] * 3 + [plane] * 4,
        in_specs=[hbm] * 12,
        out_specs=[vmem] * 7,
        scratch_shapes=scratch,
        compiler_params=pltpu.CompilerParams(
            collective_id=0, has_side_effects=True, vmem_limit_bytes=60 * 1024 * 1024
        ),
    )(*args)
    wet = (jnp.arange(levels, dtype=f32)[:, None, None] < depth[None]).astype(f32)
    return wet * tracer, east + wet * grad_e, north + wet * grad_n, solved


def solution(mesh):
    volume = P("groups", "gx", "gy")
    plane = P(("groups", "gx"), "gy")
    return jax.shard_map(
        functools.partial(per_device, mesh.shape["gx"]),
        mesh=mesh,
        in_specs=(volume,) * 6 + (P(), P("gy")) + (plane,) * 4,
        out_specs=(volume,) * 3 + (plane,),
        check_vma=False,
    )
```

```python
import functools

import jax
import jax.numpy as jnp
from jax import lax
from jax.experimental import pallas as pl
from jax.experimental.pallas import tpu as pltpu
from jax.sharding import PartitionSpec as P

SUB = 3
STIFFNESS = 0.1
WINDOW = 6
MESH = pl.DeviceIdType.MESH


def kernel(
    count_x,
    tracer_hbm, east_hbm, north_hbm, flow_e_hbm, flow_n_hbm, mixing_hbm, buoyancy_hbm, coriolis_hbm,
    depth_hbm, adj_surface_hbm, surface_diag_hbm, prior_hbm,
    tracer_out, east_out, north_out, planes_out,
    tracer_in, east_in, north_in, flow_e, flow_n, mixing, buoyancy, coriolis,
    depth_in, adj_surface, surface_diag, prior,
    rows_send, rows_recv,
    corner_send, corner_recv,
    side_recv,
    plane_rows_send, plane_rows_recv, plane_corner_recv, plane_side_send, plane_side_recv,
    sum_rows_send, sum_rows_recv, sum_corner_recv, sum_side_send, sum_side_recv,
    columns, moments, moved, load_sem, store_sem,
    rows_ss, rows_rs, corner_ss, corner_rs, side_ss, side_rs,
    plane_ss, plane_rs, sum_ss, sum_rs, moment_ss, moment_rs,
):
    levels, cols, lanes = tracer_in.shape
    wide = lanes + 128
    tall = cols + 8
    group = lax.axis_index("groups")
    gx = lax.axis_index("gx")
    gy = lax.axis_index("gy")
    other = 1 - gy
    east_of = lax.rem(gx + 1, count_x)
    west_of = lax.rem(gx + count_x - 1, count_x)
    targets = (west_of, east_of)
    edge = pl.multiple_of(other * (lanes - 128), 128)
    me = gx * 2 + gy
    peers = 2 * count_x
    window = min(WINDOW, levels)

    barrier = pltpu.get_barrier_semaphore()

    @pl.loop(1, peers)
    def _(step):
        peer = lax.rem(me + step, peers)
        pl.semaphore_signal(
            barrier, inc=1, device_id=(group, peer // 2, lax.rem(peer, 2)), device_id_type=MESH
        )

    fields_hbm = (tracer_hbm, east_hbm, north_hbm, mixing_hbm, flow_e_hbm, flow_n_hbm)
    small = [
        pltpu.make_async_copy(src, dst, load_sem.at[i])
        for i, (src, dst) in enumerate([
            (depth_hbm, depth_in), (adj_surface_hbm, adj_surface), (surface_diag_hbm, surface_diag),
            (prior_hbm, prior), (coriolis_hbm, coriolis), (buoyancy_hbm, buoyancy),
        ])
    ]
    large = [
        pltpu.make_async_copy(src, dst, load_sem.at[6 + i])
        for i, (src, dst) in enumerate(zip(fields_hbm, (tracer_in, east_in, north_in, mixing, flow_e, flow_n)))
    ]
    for copy in small + large:
        copy.start()

    sub8 = lax.broadcasted_iota(jnp.int32, (8, 1), 0)
    lane128 = lax.broadcasted_iota(jnp.int32, (1, 128), 1)

    def roll(x, shift, axis):
        return pltpu.roll(x, shift % x.shape[axis], axis)

    for copy in small:
        copy.wait()

    row = lax.broadcasted_iota(jnp.int32, (1, lanes), 1) + gy * lanes
    inside = ((row > 0) & (row < 2 * lanes - 1)).astype(jnp.float32)
    depth_own = depth_in[...].astype(jnp.float32) * inside
    planes = (depth_own, adj_surface[...], surface_diag[...], prior[...])

    def pack_pair(first, second, side):
        if side == 0:
            return jnp.where(sub8 < 4, first[:8], roll(second[:8], 4, 0))
        return jnp.where(sub8 >= 4, first[-8:], roll(second[-8:], 4, 0))

    for side in range(2):
        plane_rows_send[side, 0:8, :] = pack_pair(planes[0], planes[1], side)
        plane_rows_send[side, 8:16, :] = pack_pair(planes[2], planes[3], side)

    def edge_tile(x):
        return jnp.where(gy == 0, x[:, lanes - 128:], x[:, :128])

    for i, plane in enumerate(planes):
        plane_side_send[i] = edge_tile(plane)
    plane_side_send[4] = jnp.broadcast_to(edge_tile(coriolis[...]), (cols, 128))

    first_lane = other * 125
    edge_lane = (lane128 >= first_lane) & (lane128 < first_lane + 3)
    corner_send[...] = jnp.zeros_like(corner_send)

    def pack_three(first, second, two, k, side):
        if side == 0:
            a, b, c = first[k, 0:8, :], second[k, 0:8, :], two[k, 0:8, :]
            return jnp.where(sub8 < 3, a, jnp.where(sub8 < 6, roll(b, 3, 0), roll(c, 6, 0)))
        a, b, c = (r[k, cols - 8:cols, :] for r in (first, second, two))
        return jnp.where(sub8 >= 5, a, jnp.where(sub8 >= 2, roll(b, 5, 0), roll(c, 2, 0)))

    def remote(src, dst, ss, rs, x, y):
        return pltpu.make_async_remote_copy(
            src_ref=src, dst_ref=dst, send_sem=ss, recv_sem=rs,
            device_id=(group, x, y), device_id_type=MESH,
        )

    def planes_copies():
        out = [remote(plane_side_send, plane_side_recv, plane_ss.at[4], plane_rs.at[4], gx, other)]
        for side in range(2):
            out.append(remote(plane_rows_send.at[side], plane_rows_recv.at[side],
                              plane_ss.at[side], plane_rs.at[side], targets[side], gy))
            out.append(remote(plane_rows_send.at[side, :, pl.ds(edge, 128)], plane_corner_recv.at[side],
                              plane_ss.at[2 + side], plane_rs.at[2 + side], targets[side], other))
        return out

    def corner_copies():
        return [remote(corner_send.at[side], corner_recv.at[side], corner_ss.at[side],
                       corner_rs.at[side], targets[side], other) for side in range(2)]

    def side_copies():
        return [remote(ref.at[:, :, pl.ds(edge, 128)], side_recv.at[i], side_ss.at[i], side_rs.at[i], gx, other)
                for i, ref in enumerate(fields_hbm)]

    def rows_copies(k):
        return [remote(rows_send.at[side, k], rows_recv.at[side, k], rows_ss.at[side, k],
                       rows_rs.at[side, k], targets[side], gy) for side in range(2)]

    def sums_copies():
        out = [remote(sum_side_send, sum_side_recv, sum_ss.at[4], sum_rs.at[4], gx, other)]
        for side in range(2):
            out.append(remote(sum_rows_send.at[side], sum_rows_recv.at[side],
                              sum_ss.at[side], sum_rs.at[side], targets[side], gy))
            out.append(remote(sum_rows_send.at[side, :, pl.ds(edge, 128)], sum_corner_recv.at[side],
                              sum_ss.at[2 + side], sum_rs.at[2 + side], targets[side], other))
        return out

    pl.semaphore_wait(barrier, peers - 1)
    for copy in planes_copies() + side_copies():
        copy.start()
    for copy in large:
        copy.wait()

    @pl.loop(0, levels)
    def _(k):
        for side in range(2):
            packed = jnp.concatenate(
                [
                    pack_three(tracer_in, east_in, flow_e, k, side),
                    pack_three(north_in, mixing, flow_n, k, side),
                ],
                axis=0,
            )
            rows_send[side, k] = packed
            tile = jnp.where(edge_lane, edge_tile(packed), 0.0)
            corner_send[side] = corner_send[side] + pltpu.roll(tile, 3 * k, 1)

    for copy in corner_copies():
        copy.start()

    @pl.loop(0, window)
    def _(k):
        for copy in rows_copies(k):
            copy.start()

    def store_copies(k):
        return [pltpu.make_async_copy(moved.at[i, k], out.at[k], store_sem.at[i, k])
                for i, out in enumerate((tracer_out, east_out, north_out))]

    columns[...] = jnp.zeros_like(columns)
    for copy in planes_copies() + corner_copies() + side_copies():
        copy.wait_recv()

    def to_east(x):
        return pltpu.roll(x, tall - 1, 0)

    def to_west(x):
        return pltpu.roll(x, 1, 0)

    def to_north(x):
        return pltpu.roll(x, wide - 1, 1)

    def to_south(x):
        return pltpu.roll(x, 1, 1)

    def assemble(own, side, halo):
        return jnp.concatenate([jnp.concatenate([own, side], axis=1), halo], axis=0)

    def halo_pair(rows, corner, first):
        e = jnp.concatenate([rows[0], corner[0]], axis=1)
        w = jnp.concatenate([rows[1], corner[1]], axis=1)
        both = jnp.where(sub8 < 4, e, w) if first else jnp.where(sub8 < 4, roll(e, 4, 0), roll(w, 4, 0))
        return both

    def plane_at(i):
        tile = slice(8 * (i // 2), 8 * (i // 2) + 8)
        halo = halo_pair(
            (plane_rows_recv[0, tile, :], plane_rows_recv[1, tile, :]),
            (plane_corner_recv[0, tile, :], plane_corner_recv[1, tile, :]),
            i % 2 == 0,
        )
        return assemble(planes[i], plane_side_recv[i], halo)

    depth = plane_at(0)
    rotation = jnp.concatenate([coriolis[...], plane_side_recv[4, 0:1, :]], axis=1)

    @pl.loop(0, levels)
    def _(k):
        for copy in rows_copies(k):
            copy.wait_recv()

        @pl.when(k + window < levels)
        def _():
            for copy in rows_copies(k):
                copy.wait_send()
            for copy in rows_copies(k + window):
                copy.start()

        back = lax.rem(128 - 3 * k, 128)
        packed = [
            jnp.concatenate([rows_recv[side, k], pltpu.roll(corner_recv[side], back, 1)], axis=1)
            for side in range(2)
        ]

        def field(ref, i, tile, shift_e, shift_w):
            e = packed[0][8 * tile:8 * tile + 8]
            w = packed[1][8 * tile:8 * tile + 8]
            halo = jnp.where(sub8 < 4, roll(e, shift_e, 0), roll(w, shift_w, 0))
            return assemble(ref[k], side_recv[i, k], halo)

        wet = (k.astype(jnp.float32) < depth).astype(jnp.float32)
        wet_e, wet_n = to_east(wet) * wet, to_north(wet) * wet
        half_mix = 0.5 * field(mixing, 3, 1, 5, 3)
        face_e = (half_mix + to_east(half_mix)) * wet_e
        face_n = (half_mix + to_north(half_mix)) * wet_n
        face_w, face_s = to_west(face_e), to_south(face_n)
        half = 0.5 * wet
        carry_e = half * field(flow_e, 4, 0, 2, 6)
        carry_n = half * field(flow_n, 5, 1, 2, 6)
        take_e, take_w = face_e + carry_e, face_w - carry_e
        take_n, take_s = face_n + carry_n, face_s - carry_n
        take = wet - (face_e + face_w) - (face_n + face_s)
        turn = wet * rotation
        lift = buoyancy[k]
        lift_e, lift_n, lift_here = lift * wet_e, lift * wet_n, lift * wet
        t = wet * field(tracer_in, 0, 0, 0, 0)
        e = wet * field(east_in, 1, 0, 5, 3)
        n = wet * field(north_in, 2, 1, 0, 0)
        for _ in range(SUB):
            e_w, n_s = to_west(e), to_south(n)
            t_new = (take * t + take_e * to_east(t) + take_w * to_west(t)
                     + take_n * to_north(t) + take_s * to_south(t)
                     + (lift_e * e + lift_n * n - lift_here * (e_w + n_s)))
            e_new = (take * e + take_e * to_east(e) + take_w * e_w
                     + take_n * to_north(e) + take_s * to_south(e) - turn * n)
            n_new = (take * n + take_e * to_east(n) + take_w * to_west(n)
                     + take_n * to_north(n) + take_s * n_s + turn * e)
            t, e, n = t_new, e_new, n_new
        own = (slice(0, cols), slice(0, lanes))
        for i, q in enumerate((t, e, n)):
            moved[i, k] = q[own]
        for copy in store_copies(k):
            copy.start()
        columns[0] = columns[0] + e[own]
        columns[1] = columns[1] + n[own]

    sum_e, sum_n = columns[0], columns[1]
    for side in range(2):
        sum_rows_send[side] = pack_pair(sum_e, sum_n, side)
    sum_side_send[0] = edge_tile(sum_e)
    sum_side_send[1] = edge_tile(sum_n)
    for copy in sums_copies():
        copy.start()

    wet_column = (depth > 0.0).astype(jnp.float32)
    reach_e = STIFFNESS * jnp.minimum(depth, to_east(depth))
    reach_n = STIFFNESS * jnp.minimum(depth, to_north(depth))
    reach_w, reach_s = to_west(reach_e), to_south(reach_n)
    centre = plane_at(2) + (reach_e + reach_w) + (reach_n + reach_s)

    def operator(p):
        return (centre * p - reach_e * to_east(p) - reach_w * to_west(p)
                - reach_n * to_north(p) - reach_s * to_south(p))

    start = wet_column * plane_at(3)
    base = wet_column * plane_at(1) - operator(start)

    for copy in sums_copies():
        copy.wait_recv()

    def sum_at(i, own):
        halo = halo_pair((sum_rows_recv[0], sum_rows_recv[1]), (sum_corner_recv[0], sum_corner_recv[1]), i == 0)
        return assemble(own, sum_side_recv[i], halo)

    all_e, all_n = sum_at(0, sum_e), sum_at(1, sum_n)
    v0 = base + (0.5 * wet_column) * (to_west(all_e) - to_east(all_e) + to_south(all_n) - to_north(all_n))
    v1 = operator(v0)
    v2 = operator(v1)
    v3 = operator(v2)

    w = [v[0:cols, 0:lanes] for v in (v0, v1, v2, v3)]

    def partial(a, b):
        s = jnp.sum((a * b).reshape(cols // 8, 8, lanes), axis=0)
        total = s[:, 0:128]
        for j in range(128, lanes, 128):
            total = total + s[:, j:j + 128]
        return jnp.sum(total, axis=0, keepdims=True)

    terms = [partial(w[0], w[0]), partial(w[0], w[1]), partial(w[1], w[1]),
             partial(w[1], w[2]), partial(w[2], w[2]), partial(w[2], w[3])]
    mine = jnp.concatenate(terms + [jnp.zeros((2, 128), jnp.float32)], axis=0)
    moments[me] = mine

    def moment_copy(step):
        peer = lax.rem(me + step, peers)
        return remote(moments.at[me], moments.at[me], moment_ss.at[step], moment_rs.at[me],
                      peer // 2, lax.rem(peer, 2))

    @pl.loop(1, peers)
    def _(step):
        moment_copy(step).start()

    @pl.loop(1, peers)
    def _(step):
        source = lax.rem(me + step, peers)
        remote(moments.at[me], moments.at[source], moment_ss.at[step], moment_rs.at[source],
               source // 2, lax.rem(source, 2)).wait_recv()

    total = jnp.sum(jnp.sum(moments[...], axis=0), axis=1, keepdims=True)
    mu = [jnp.broadcast_to(total[m:m + 1, :], (1, 128)) for m in range(6)]

    def form(c, at):
        out = 0.0
        for i, a in enumerate(c):
            for j, b in enumerate(c):
                out = out + a * b * mu[at + i + j]
        return out

    r = [jnp.ones((1, 128), jnp.float32)]
    d = list(r)
    rr = mu[0]
    gain = [jnp.zeros((1, 128), jnp.float32) for _ in range(3)]
    for iteration in range(3):
        alpha = rr / form(d, 1)
        for i in range(len(d)):
            gain[i] = gain[i] + alpha * d[i]
        if iteration < 2:
            shifted = [jnp.zeros((1, 128), jnp.float32)] + d
            r = [a - alpha * b for a, b in zip(r + [jnp.zeros((1, 128), jnp.float32)], shifted)]
            new = form(r, 0)
            beta = new / rr
            d = [a + beta * b for a, b in zip(r, d + [jnp.zeros((1, 128), jnp.float32)])]
            rr = new
    gain = [g[:, 0:1] for g in gain]
    solved = start + gain[0] * v0 + gain[1] * v1 + gain[2] * v2
    planes_out[0] = (0.5 * (to_east(solved) - to_west(solved)))[0:cols, 0:lanes]
    planes_out[1] = (0.5 * (to_north(solved) - to_south(solved)))[0:cols, 0:lanes]
    planes_out[2] = depth_own
    planes_out[3] = solved[0:cols, 0:lanes]

    @pl.loop(0, levels)
    def _(k):
        for copy in store_copies(k):
            copy.wait()

    for copy in planes_copies() + corner_copies() + side_copies() + sums_copies():
        copy.wait_send()

    @pl.loop(levels - window, levels)
    def _(k):
        for copy in rows_copies(k):
            copy.wait_send()

    @pl.loop(1, peers)
    def _(step):
        moment_copy(step).wait_send()


def finish(
    tracer_in, east_in, north_in, planes_in, tracer_out, east_out, north_out, solution_out,
    tracer, east, north, planes, load_sem, store_sem,
):
    levels = tracer_in.shape[0]
    parts = [pl.ds(0, levels // 2), pl.ds(levels // 2, levels - levels // 2)]
    pairs = [(east_in, east, east_out), (north_in, north, north_out)]
    first = pltpu.make_async_copy(planes_in, planes, load_sem.at[0])
    last = pltpu.make_async_copy(tracer_in, tracer, load_sem.at[1])
    loads = [pltpu.make_async_copy(src.at[part], held.at[part], load_sem.at[2 + 2 * i + j])
             for i, part in enumerate(parts) for j, (src, held, _) in enumerate(pairs)]
    stores = [pltpu.make_async_copy(held.at[part], dst.at[part], store_sem.at[2 + 2 * i + j])
              for i, part in enumerate(parts) for j, (_, held, dst) in enumerate(pairs)]
    whole = [pltpu.make_async_copy(planes.at[3], solution_out, store_sem.at[0]),
             pltpu.make_async_copy(tracer, tracer_out, store_sem.at[1])]
    for copy in [first] + loads + [last]:
        copy.start()
    first.wait()
    whole[0].start()
    depth = planes[2]
    for i, part in enumerate(parts):
        for j, (_, held, _) in enumerate(pairs):
            loads[2 * i + j].wait()
            for k in range(part.start, part.start + part.size):
                held[k] = held[k] + jnp.where(depth > float(k), planes[j], 0.0)
            stores[2 * i + j].start()
    last.wait()
    whole[1].start()
    for copy in whole + stores:
        copy.wait()


def per_device(count_x, *args):
    levels, cols, lanes = args[0].shape
    args = list(args)
    args[7] = args[7].reshape(1, lanes)
    f32 = jnp.float32
    vmem = pl.BlockSpec(memory_space=pltpu.VMEM)
    hbm = pl.BlockSpec(memory_space=pltpu.HBM)
    peers = 2 * count_x
    dma = pltpu.SemaphoreType.DMA
    scratch = [pltpu.VMEM((levels, cols, lanes), f32)] * 6 + [
        pltpu.SMEM((levels,), f32), pltpu.VMEM((1, lanes), f32), pltpu.VMEM((cols, lanes), args[8].dtype),
    ] + [pltpu.VMEM((cols, lanes), f32)] * 3 + [
        pltpu.VMEM((2, levels, 16, lanes), f32), pltpu.VMEM((2, levels, 16, lanes), f32),
        pltpu.VMEM((2, 16, 128), f32), pltpu.VMEM((2, 16, 128), f32),
        pltpu.VMEM((6, levels, cols, 128), f32),
        pltpu.VMEM((2, 16, lanes), f32), pltpu.VMEM((2, 16, lanes), f32), pltpu.VMEM((2, 16, 128), f32),
        pltpu.VMEM((5, cols, 128), f32), pltpu.VMEM((5, cols, 128), f32),
        pltpu.VMEM((2, 8, lanes), f32), pltpu.VMEM((2, 8, lanes), f32), pltpu.VMEM((2, 8, 128), f32),
        pltpu.VMEM((2, cols, 128), f32), pltpu.VMEM((2, cols, 128), f32),
        pltpu.VMEM((2, cols, lanes), f32), pltpu.VMEM((peers, 8, 128), f32),
        pltpu.VMEM((3, levels, cols, lanes), f32), dma((12,)), dma((3, levels)),
        dma((2, levels)), dma((2, levels)), dma((2,)), dma((2,)), dma((6,)), dma((6,)),
        dma((5,)), dma((5,)), dma((5,)), dma((5,)), dma((peers,)), dma((peers,)),
    ]
    volume = jax.ShapeDtypeStruct((levels, cols, lanes), f32)
    plane = jax.ShapeDtypeStruct((cols, lanes), f32)
    tracer, east, north, planes = pl.pallas_call(
        functools.partial(kernel, count_x),
        out_shape=[volume] * 3 + [jax.ShapeDtypeStruct((4, cols, lanes), f32)],
        in_specs=[hbm] * 12,
        out_specs=[hbm] * 3 + [vmem],
        scratch_shapes=scratch,
        compiler_params=pltpu.CompilerParams(
            collective_id=0, has_side_effects=True, vmem_limit_bytes=60 * 1024 * 1024
        ),
    )(*args)
    return pl.pallas_call(
        finish,
        out_shape=[volume] * 3 + [plane],
        in_specs=[hbm] * 4,
        out_specs=[hbm] * 4,
        scratch_shapes=[pltpu.VMEM((levels, cols, lanes), f32)] * 3 + [
            pltpu.VMEM((4, cols, lanes), f32), dma((6,)), dma((6,)),
        ],
        compiler_params=pltpu.CompilerParams(vmem_limit_bytes=60 * 1024 * 1024),
    )(tracer, east, north, planes)


def solution(mesh):
    volume = P("groups", "gx", "gy")
    plane = P(("groups", "gx"), "gy")
    return jax.shard_map(
        functools.partial(per_device, mesh.shape["gx"]),
        mesh=mesh,
        in_specs=(volume,) * 6 + (P(), P("gy")) + (plane,) * 4,
        out_specs=(volume,) * 3 + (plane,),
        check_vma=False,
    )
```

```python
import functools

import jax
import jax.numpy as jnp
from jax import lax
from jax.experimental import pallas as pl
from jax.experimental.pallas import tpu as pltpu
from jax.sharding import PartitionSpec as P

SUB = 3
STIFFNESS = 0.1
WINDOW = 6
MESH = pl.DeviceIdType.MESH


def kernel(
    count_x,
    tracer_hbm, east_hbm, north_hbm, flow_e_hbm, flow_n_hbm, mixing_hbm, buoyancy_hbm, coriolis_hbm,
    depth_hbm, adj_surface_hbm, surface_diag_hbm, prior_hbm,
    tracer_out, east_out, north_out, planes_out,
    tracer_in, east_in, north_in, flow_e, flow_n, mixing, buoyancy, coriolis,
    depth_in, adj_surface, surface_diag, prior,
    rows_send, rows_recv,
    corner_send, corner_recv,
    side_recv,
    plane_rows_send, plane_rows_recv, plane_corner_recv, plane_side_send, plane_side_recv,
    sum_rows_send, sum_rows_recv, sum_corner_recv, sum_side_send, sum_side_recv,
    columns, moments, moved, load_sem, store_sem,
    rows_ss, rows_rs, corner_ss, corner_rs, side_ss, side_rs,
    plane_ss, plane_rs, sum_ss, sum_rs, moment_ss, moment_rs,
):
    levels, cols, lanes = tracer_in.shape
    wide = lanes + 128
    tall = cols + 8
    group = lax.axis_index("groups")
    gx = lax.axis_index("gx")
    gy = lax.axis_index("gy")
    other = 1 - gy
    east_of = lax.rem(gx + 1, count_x)
    west_of = lax.rem(gx + count_x - 1, count_x)
    targets = (west_of, east_of)
    edge = pl.multiple_of(other * (lanes - 128), 128)
    me = gx * 2 + gy
    peers = 2 * count_x
    window = min(WINDOW, levels)

    barrier = pltpu.get_barrier_semaphore()

    @pl.loop(1, peers)
    def _(step):
        peer = lax.rem(me + step, peers)
        pl.semaphore_signal(
            barrier, inc=1, device_id=(group, peer // 2, lax.rem(peer, 2)), device_id_type=MESH
        )

    fields_hbm = (tracer_hbm, east_hbm, north_hbm, mixing_hbm, flow_e_hbm, flow_n_hbm)
    small = [
        pltpu.make_async_copy(src, dst, load_sem.at[i])
        for i, (src, dst) in enumerate([
            (depth_hbm, depth_in), (adj_surface_hbm, adj_surface), (surface_diag_hbm, surface_diag),
            (prior_hbm, prior), (coriolis_hbm, coriolis), (buoyancy_hbm, buoyancy),
        ])
    ]
    large = [
        pltpu.make_async_copy(src, dst, load_sem.at[6 + i])
        for i, (src, dst) in enumerate(zip(fields_hbm, (tracer_in, east_in, north_in, mixing, flow_e, flow_n)))
    ]
    for copy in small + large:
        copy.start()

    sub8 = lax.broadcasted_iota(jnp.int32, (8, 1), 0)
    lane128 = lax.broadcasted_iota(jnp.int32, (1, 128), 1)

    def roll(x, shift, axis):
        return pltpu.roll(x, shift % x.shape[axis], axis)

    for copy in small:
        copy.wait()

    row = lax.broadcasted_iota(jnp.int32, (1, lanes), 1) + gy * lanes
    inside = ((row > 0) & (row < 2 * lanes - 1)).astype(jnp.float32)
    depth_own = depth_in[...].astype(jnp.float32) * inside
    planes = (depth_own, adj_surface[...], surface_diag[...], prior[...])

    def pack_pair(first, second, side):
        if side == 0:
            return jnp.where(sub8 < 4, first[:8], roll(second[:8], 4, 0))
        return jnp.where(sub8 >= 4, first[-8:], roll(second[-8:], 4, 0))

    for side in range(2):
        plane_rows_send[side, 0:8, :] = pack_pair(planes[0], planes[1], side)
        plane_rows_send[side, 8:16, :] = pack_pair(planes[2], planes[3], side)

    def edge_tile(x):
        return jnp.where(gy == 0, x[:, lanes - 128:], x[:, :128])

    for i, plane in enumerate(planes):
        plane_side_send[i] = edge_tile(plane)
    plane_side_send[4] = jnp.broadcast_to(edge_tile(coriolis[...]), (cols, 128))

    first_lane = other * 125
    edge_lane = (lane128 >= first_lane) & (lane128 < first_lane + 3)
    corner_send[...] = jnp.zeros_like(corner_send)

    def pack_three(first, second, two, k, side):
        if side == 0:
            a, b, c = first[k, 0:8, :], second[k, 0:8, :], two[k, 0:8, :]
            return jnp.where(sub8 < 3, a, jnp.where(sub8 < 6, roll(b, 3, 0), roll(c, 6, 0)))
        a, b, c = (r[k, cols - 8:cols, :] for r in (first, second, two))
        return jnp.where(sub8 >= 5, a, jnp.where(sub8 >= 2, roll(b, 5, 0), roll(c, 2, 0)))

    def remote(src, dst, ss, rs, x, y):
        return pltpu.make_async_remote_copy(
            src_ref=src, dst_ref=dst, send_sem=ss, recv_sem=rs,
            device_id=(group, x, y), device_id_type=MESH,
        )

    def planes_copies():
        out = [remote(plane_side_send, plane_side_recv, plane_ss.at[4], plane_rs.at[4], gx, other)]
        for side in range(2):
            out.append(remote(plane_rows_send.at[side], plane_rows_recv.at[side],
                              plane_ss.at[side], plane_rs.at[side], targets[side], gy))
            out.append(remote(plane_rows_send.at[side, :, pl.ds(edge, 128)], plane_corner_recv.at[side],
                              plane_ss.at[2 + side], plane_rs.at[2 + side], targets[side], other))
        return out

    def corner_copies():
        return [remote(corner_send.at[side], corner_recv.at[side], corner_ss.at[side],
                       corner_rs.at[side], targets[side], other) for side in range(2)]

    def side_copies():
        return [remote(ref.at[:, :, pl.ds(edge, 128)], side_recv.at[i], side_ss.at[i], side_rs.at[i], gx, other)
                for i, ref in enumerate(fields_hbm)]

    def rows_copies(k):
        return [remote(rows_send.at[side, k], rows_recv.at[side, k], rows_ss.at[side, k],
                       rows_rs.at[side, k], targets[side], gy) for side in range(2)]

    def sums_copies():
        out = [remote(sum_side_send, sum_side_recv, sum_ss.at[4], sum_rs.at[4], gx, other)]
        for side in range(2):
            out.append(remote(sum_rows_send.at[side], sum_rows_recv.at[side],
                              sum_ss.at[side], sum_rs.at[side], targets[side], gy))
            out.append(remote(sum_rows_send.at[side, :, pl.ds(edge, 128)], sum_corner_recv.at[side],
                              sum_ss.at[2 + side], sum_rs.at[2 + side], targets[side], other))
        return out

    pl.semaphore_wait(barrier, peers - 1)
    for copy in planes_copies() + side_copies():
        copy.start()
    for copy in large:
        copy.wait()

    @pl.loop(0, levels)
    def _(k):
        for side in range(2):
            packed = jnp.concatenate(
                [
                    pack_three(tracer_in, east_in, flow_e, k, side),
                    pack_three(north_in, mixing, flow_n, k, side),
                ],
                axis=0,
            )
            rows_send[side, k] = packed
            tile = jnp.where(edge_lane, edge_tile(packed), 0.0)
            corner_send[side] = corner_send[side] + pltpu.roll(tile, 3 * k, 1)

    for copy in corner_copies():
        copy.start()

    @pl.loop(0, window)
    def _(k):
        for copy in rows_copies(k):
            copy.start()

    def store_copies(k):
        return [pltpu.make_async_copy(moved.at[i, k], out.at[k], store_sem.at[i, k])
                for i, out in enumerate((tracer_out, east_out, north_out))]

    columns[...] = jnp.zeros_like(columns)
    for copy in planes_copies() + corner_copies() + side_copies():
        copy.wait_recv()

    def to_east(x):
        return pltpu.roll(x, tall - 1, 0)

    def to_west(x):
        return pltpu.roll(x, 1, 0)

    def to_north(x):
        return pltpu.roll(x, wide - 1, 1)

    def to_south(x):
        return pltpu.roll(x, 1, 1)

    def assemble(own, side, halo):
        return jnp.concatenate([jnp.concatenate([own, side], axis=1), halo], axis=0)

    def halo_pair(rows, corner, first):
        e = jnp.concatenate([rows[0], corner[0]], axis=1)
        w = jnp.concatenate([rows[1], corner[1]], axis=1)
        both = jnp.where(sub8 < 4, e, w) if first else jnp.where(sub8 < 4, roll(e, 4, 0), roll(w, 4, 0))
        return both

    def plane_at(i):
        tile = slice(8 * (i // 2), 8 * (i // 2) + 8)
        halo = halo_pair(
            (plane_rows_recv[0, tile, :], plane_rows_recv[1, tile, :]),
            (plane_corner_recv[0, tile, :], plane_corner_recv[1, tile, :]),
            i % 2 == 0,
        )
        return assemble(planes[i], plane_side_recv[i], halo)

    depth = plane_at(0)
    rotation = jnp.concatenate([coriolis[...], plane_side_recv[4, 0:1, :]], axis=1)

    @pl.loop(0, levels)
    def _(k):
        for copy in rows_copies(k):
            copy.wait_recv()

        @pl.when(k + window < levels)
        def _():
            for copy in rows_copies(k):
                copy.wait_send()
            for copy in rows_copies(k + window):
                copy.start()

        back = lax.rem(128 - 3 * k, 128)
        packed = [
            jnp.concatenate([rows_recv[side, k], pltpu.roll(corner_recv[side], back, 1)], axis=1)
            for side in range(2)
        ]

        def field(ref, i, tile, shift_e, shift_w):
            e = packed[0][8 * tile:8 * tile + 8]
            w = packed[1][8 * tile:8 * tile + 8]
            halo = jnp.where(sub8 < 4, roll(e, shift_e, 0), roll(w, shift_w, 0))
            return assemble(ref[k], side_recv[i, k], halo)

        wet = (k.astype(jnp.float32) < depth).astype(jnp.float32)
        wet_e, wet_n = to_east(wet) * wet, to_north(wet) * wet
        half_mix = 0.5 * field(mixing, 3, 1, 5, 3)
        face_e = (half_mix + to_east(half_mix)) * wet_e
        face_n = (half_mix + to_north(half_mix)) * wet_n
        face_w, face_s = to_west(face_e), to_south(face_n)
        half = 0.5 * wet
        carry_e = half * field(flow_e, 4, 0, 2, 6)
        carry_n = half * field(flow_n, 5, 1, 2, 6)
        take_e, take_w = face_e + carry_e, face_w - carry_e
        take_n, take_s = face_n + carry_n, face_s - carry_n
        take = wet - (face_e + face_w) - (face_n + face_s)
        turn = wet * rotation
        lift = buoyancy[k]
        lift_e, lift_n, lift_here = lift * wet_e, lift * wet_n, lift * wet
        t = wet * field(tracer_in, 0, 0, 0, 0)
        e = wet * field(east_in, 1, 0, 5, 3)
        n = wet * field(north_in, 2, 1, 0, 0)
        for _ in range(SUB):
            e_w, n_s = to_west(e), to_south(n)
            t_new = (take * t + take_e * to_east(t) + take_w * to_west(t)
                     + take_n * to_north(t) + take_s * to_south(t)
                     + (lift_e * e + lift_n * n - lift_here * (e_w + n_s)))
            e_new = (take * e + take_e * to_east(e) + take_w * e_w
                     + take_n * to_north(e) + take_s * to_south(e) - turn * n)
            n_new = (take * n + take_e * to_east(n) + take_w * to_west(n)
                     + take_n * to_north(n) + take_s * n_s + turn * e)
            t, e, n = t_new, e_new, n_new
        own = (slice(0, cols), slice(0, lanes))
        for i, q in enumerate((t, e, n)):
            moved[i, k] = q[own]
        for copy in store_copies(k):
            copy.start()
        columns[0] = columns[0] + e[own]
        columns[1] = columns[1] + n[own]

    sum_e, sum_n = columns[0], columns[1]
    for side in range(2):
        sum_rows_send[side] = pack_pair(sum_e, sum_n, side)
    sum_side_send[0] = edge_tile(sum_e)
    sum_side_send[1] = edge_tile(sum_n)
    for copy in sums_copies():
        copy.start()

    wet_column = (depth > 0.0).astype(jnp.float32)
    reach_e = STIFFNESS * jnp.minimum(depth, to_east(depth))
    reach_n = STIFFNESS * jnp.minimum(depth, to_north(depth))
    reach_w, reach_s = to_west(reach_e), to_south(reach_n)
    centre = plane_at(2) + (reach_e + reach_w) + (reach_n + reach_s)

    def operator(p):
        return (centre * p - reach_e * to_east(p) - reach_w * to_west(p)
                - reach_n * to_north(p) - reach_s * to_south(p))

    start = wet_column * plane_at(3)
    base = wet_column * plane_at(1) - operator(start)

    for copy in sums_copies():
        copy.wait_recv()

    def sum_at(i, own):
        halo = halo_pair((sum_rows_recv[0], sum_rows_recv[1]), (sum_corner_recv[0], sum_corner_recv[1]), i == 0)
        return assemble(own, sum_side_recv[i], halo)

    all_e, all_n = sum_at(0, sum_e), sum_at(1, sum_n)
    v0 = base + (0.5 * wet_column) * (to_west(all_e) - to_east(all_e) + to_south(all_n) - to_north(all_n))
    v1 = operator(v0)
    v2 = operator(v1)
    v3 = operator(v2)

    w = [v[0:cols, 0:lanes] for v in (v0, v1, v2, v3)]

    def partial(a, b):
        s = jnp.sum((a * b).reshape(cols // 8, 8, lanes), axis=0)
        total = s[:, 0:128]
        for j in range(128, lanes, 128):
            total = total + s[:, j:j + 128]
        return jnp.sum(total, axis=0, keepdims=True)

    terms = [partial(w[0], w[0]), partial(w[0], w[1]), partial(w[1], w[1]),
             partial(w[1], w[2]), partial(w[2], w[2]), partial(w[2], w[3])]
    mine = jnp.concatenate(terms + [jnp.zeros((2, 128), jnp.float32)], axis=0)
    moments[me] = mine

    def moment_copy(step):
        peer = lax.rem(me + step, peers)
        return remote(moments.at[me], moments.at[me], moment_ss.at[step], moment_rs.at[me],
                      peer // 2, lax.rem(peer, 2))

    @pl.loop(1, peers)
    def _(step):
        moment_copy(step).start()

    @pl.loop(0, levels)
    def _(k):
        for copy in store_copies(k):
            copy.wait()

    for copy in planes_copies() + corner_copies() + side_copies() + sums_copies():
        copy.wait_send()

    @pl.loop(levels - window, levels)
    def _(k):
        for copy in rows_copies(k):
            copy.wait_send()

    @pl.loop(1, peers)
    def _(step):
        source = lax.rem(me + step, peers)
        remote(moments.at[me], moments.at[source], moment_ss.at[step], moment_rs.at[source],
               source // 2, lax.rem(source, 2)).wait_recv()

    total = jnp.sum(jnp.sum(moments[...], axis=0), axis=1, keepdims=True)
    mu = [jnp.broadcast_to(total[m:m + 1, :], (1, 128)) for m in range(6)]

    def form(c, at):
        out = 0.0
        for i, a in enumerate(c):
            for j, b in enumerate(c):
                out = out + a * b * mu[at + i + j]
        return out

    r = [jnp.ones((1, 128), jnp.float32)]
    d = list(r)
    rr = mu[0]
    gain = [jnp.zeros((1, 128), jnp.float32) for _ in range(3)]
    for iteration in range(3):
        alpha = rr / form(d, 1)
        for i in range(len(d)):
            gain[i] = gain[i] + alpha * d[i]
        if iteration < 2:
            shifted = [jnp.zeros((1, 128), jnp.float32)] + d
            r = [a - alpha * b for a, b in zip(r + [jnp.zeros((1, 128), jnp.float32)], shifted)]
            new = form(r, 0)
            beta = new / rr
            d = [a + beta * b for a, b in zip(r, d + [jnp.zeros((1, 128), jnp.float32)])]
            rr = new
    gain = [g[:, 0:1] for g in gain]
    solved = start + gain[0] * v0 + gain[1] * v1 + gain[2] * v2
    planes_out[0] = (0.5 * (to_east(solved) - to_west(solved)))[0:cols, 0:lanes]
    planes_out[1] = (0.5 * (to_north(solved) - to_south(solved)))[0:cols, 0:lanes]
    planes_out[2] = depth_own
    planes_out[3] = solved[0:cols, 0:lanes]

    @pl.loop(1, peers)
    def _(step):
        moment_copy(step).wait_send()


def finish(
    tracer_in, east_in, north_in, planes_in, tracer_out, east_out, north_out, solution_out,
    tracer, east, north, planes, load_sem, store_sem,
):
    levels = tracer_in.shape[0]
    parts = [pl.ds(0, levels // 2), pl.ds(levels // 2, levels - levels // 2)]
    pairs = [(east_in, east, east_out), (north_in, north, north_out)]
    first = pltpu.make_async_copy(planes_in, planes, load_sem.at[0])
    last = pltpu.make_async_copy(tracer_in, tracer, load_sem.at[1])
    loads = [pltpu.make_async_copy(src.at[part], held.at[part], load_sem.at[2 + 2 * i + j])
             for i, part in enumerate(parts) for j, (src, held, _) in enumerate(pairs)]
    stores = [pltpu.make_async_copy(held.at[part], dst.at[part], store_sem.at[2 + 2 * i + j])
              for i, part in enumerate(parts) for j, (_, held, dst) in enumerate(pairs)]
    whole = [pltpu.make_async_copy(planes.at[3], solution_out, store_sem.at[0]),
             pltpu.make_async_copy(tracer, tracer_out, store_sem.at[1])]
    for copy in [first] + loads + [last]:
        copy.start()
    first.wait()
    whole[0].start()
    depth = planes[2]
    for i, part in enumerate(parts):
        for j, (_, held, _) in enumerate(pairs):
            loads[2 * i + j].wait()
            for k in range(part.start, part.start + part.size):
                held[k] = held[k] + jnp.where(depth > float(k), planes[j], 0.0)
            stores[2 * i + j].start()
    last.wait()
    whole[1].start()
    for copy in whole + stores:
        copy.wait()


def per_device(count_x, *args):
    levels, cols, lanes = args[0].shape
    args = list(args)
    args[7] = args[7].reshape(1, lanes)
    f32 = jnp.float32
    vmem = pl.BlockSpec(memory_space=pltpu.VMEM)
    hbm = pl.BlockSpec(memory_space=pltpu.HBM)
    peers = 2 * count_x
    dma = pltpu.SemaphoreType.DMA
    scratch = [pltpu.VMEM((levels, cols, lanes), f32)] * 6 + [
        pltpu.SMEM((levels,), f32), pltpu.VMEM((1, lanes), f32), pltpu.VMEM((cols, lanes), args[8].dtype),
    ] + [pltpu.VMEM((cols, lanes), f32)] * 3 + [
        pltpu.VMEM((2, levels, 16, lanes), f32), pltpu.VMEM((2, levels, 16, lanes), f32),
        pltpu.VMEM((2, 16, 128), f32), pltpu.VMEM((2, 16, 128), f32),
        pltpu.VMEM((6, levels, cols, 128), f32),
        pltpu.VMEM((2, 16, lanes), f32), pltpu.VMEM((2, 16, lanes), f32), pltpu.VMEM((2, 16, 128), f32),
        pltpu.VMEM((5, cols, 128), f32), pltpu.VMEM((5, cols, 128), f32),
        pltpu.VMEM((2, 8, lanes), f32), pltpu.VMEM((2, 8, lanes), f32), pltpu.VMEM((2, 8, 128), f32),
        pltpu.VMEM((2, cols, 128), f32), pltpu.VMEM((2, cols, 128), f32),
        pltpu.VMEM((2, cols, lanes), f32), pltpu.VMEM((peers, 8, 128), f32),
        pltpu.VMEM((3, levels, cols, lanes), f32), dma((12,)), dma((3, levels)),
        dma((2, levels)), dma((2, levels)), dma((2,)), dma((2,)), dma((6,)), dma((6,)),
        dma((5,)), dma((5,)), dma((5,)), dma((5,)), dma((peers,)), dma((peers,)),
    ]
    volume = jax.ShapeDtypeStruct((levels, cols, lanes), f32)
    plane = jax.ShapeDtypeStruct((cols, lanes), f32)
    tracer, east, north, planes = pl.pallas_call(
        functools.partial(kernel, count_x),
        out_shape=[volume] * 3 + [jax.ShapeDtypeStruct((4, cols, lanes), f32)],
        in_specs=[hbm] * 12,
        out_specs=[hbm] * 3 + [vmem],
        scratch_shapes=scratch,
        compiler_params=pltpu.CompilerParams(
            collective_id=0, has_side_effects=True, vmem_limit_bytes=60 * 1024 * 1024
        ),
    )(*args)
    return pl.pallas_call(
        finish,
        out_shape=[volume] * 3 + [plane],
        in_specs=[hbm] * 4,
        out_specs=[hbm] * 4,
        scratch_shapes=[pltpu.VMEM((levels, cols, lanes), f32)] * 3 + [
            pltpu.VMEM((4, cols, lanes), f32), dma((6,)), dma((6,)),
        ],
        compiler_params=pltpu.CompilerParams(vmem_limit_bytes=60 * 1024 * 1024),
    )(tracer, east, north, planes)


def solution(mesh):
    volume = P("groups", "gx", "gy")
    plane = P(("groups", "gx"), "gy")
    return jax.shard_map(
        functools.partial(per_device, mesh.shape["gx"]),
        mesh=mesh,
        in_specs=(volume,) * 6 + (P(), P("gy")) + (plane,) * 4,
        out_specs=(volume,) * 3 + (plane,),
        check_vma=False,
    )
```
